32 devices in a mesh: row: 4 (over z), col: 8 (over y, x, core).
Axes of the slice: x: 2, y: 2, z: 4, core: 2. Of those that a mesh axis runs over, the one named last changes fastest.
Arguments:
- primal: float32 [8, 32768], P(None, ('col', 'row')), may hold values from 0 to 0.5
- dual: float32 [8, 32768], P(None, ('row', 'col')), may hold values from 0 to 1
- cost: float32 [8, 32768], P(None, ('col', 'row')), may hold values from -6 to 6
- upper: float32 [32768], P(('col', 'row')), may hold values from 0.25 to 1.5
- rhs: float32 [32768], P(('row', 'col')), may hold values from -6 to 6
- row_kind: int32 [32768], P(('row', 'col')), may hold values 0 or 1
- tiles: bfloat16 [1536, 128, 128], P(('row', 'col')), may hold values from -0.25 to 0.25
- tile_rows: int32 [1536], P(('row', 'col')), may hold values from 0 to 63, as said below
- tile_cols: int32 [1536], P(('row', 'col')), may hold values from 0 to 31
- tile_count: int32 [32], P(('row', 'col')), may hold values from 1 to 48, as said below
Outputs:
- primal_out: float32 [8, 32768], P(None, ('col', 'row'))
- dual_out: float32 [8, 32768], P(None, ('row', 'col'))
The draws below stay inside these ranges and needn't reach their ends.
Inputs may be any that keep to these rules, and one draw needn't show every extreme that they name: Within one device's slots the pairs (tile_rows, tile_cols) are all different. `tile_count`: some device has all 48 slots live in every draw; which one varies.
All inputs are finite; a program needn't handle non-finite values. No bound on the sum of `row_kind` on one device may be relied on, other than what follows from the above.
Results may differ from the reference program's by a relative error of at most 0.0012.
Values may be sent and summed in bfloat16 or wider, within the bound.
A program may use at most 64 MiB of HBM per device.

```python
import jax
import jax.numpy as jnp
from jax import lax

REALIZATIONS = 8
ROWT = 64
COLT = 32
TILES_DEV = 48
ITERS = 2
NVAR = 32768
NCON = 32768
N_ROW = 4
N_COL = 8


def tile_positions(key):
    keys = jax.random.split(key, N_ROW * N_COL)

    def one_device(single):
        return jax.random.permutation(single, ROWT * COLT)[:TILES_DEV]
    return jax.vmap(one_device)(keys).reshape(-1).astype(jnp.int32)


def draw_tile_rows(key, part):
    return (tile_positions(key) // COLT).astype(jnp.int32)


def draw_tile_cols(key, part):
    return (tile_positions(key) % COLT).astype(jnp.int32)


def draw_tile_count(key, part):
    key = jax.random.fold_in(key, 5)
    first_key, second_key = jax.random.split(key)
    lowest = max(1, TILES_DEV // 4)
    counts = jax.random.randint(first_key, (N_ROW * N_COL,), lowest, TILES_DEV + 1)
    busiest = jax.random.randint(second_key, (), 0, N_ROW * N_COL)
    return counts.at[busiest].set(TILES_DEV).astype(jnp.int32)


def set_ends(result, own_key, smallest, largest):
    spot = [jax.random.randint(jax.random.fold_in(own_key, axis), (), 0, length) for axis, length in enumerate(result.shape)]
    widest = result.shape.index(max(result.shape))
    beside = spot[:widest] + [(spot[widest] + 1) % result.shape[widest]] + spot[widest + 1:]
    return result.at[tuple(spot)].set(smallest).at[tuple(beside)].set(largest)


def steps_of(key, shape, cuts, least, largest):
    loudness = 1.0
    for dim, parts in cuts:
        steps = jax.random.uniform(jax.random.fold_in(jax.random.fold_in(key, 6), dim), (parts,), jnp.float32, least / len(cuts), largest / len(cuts))
        loudness = loudness * jnp.repeat(jnp.exp(steps), shape[dim] // parts).reshape((-1,) + (1,) * (len(shape) - 1 - dim))
    return loudness


def normal_values(rng, extent, scale, bound, cuts=(), held_as=jnp.bfloat16):
    result = jax.random.normal(rng, extent, jnp.float32) * scale
    if len(cuts) > 0:
        result = steps_of(rng, extent, cuts, -0.22, 0.18) * result
    return jnp.clip(result, min=-bound, max=bound).astype(held_as)


def setup_inputs(seed: int = 0) -> dict:
    key_list = jax.random.split(jax.random.key(seed), 11)
    return {
        "primal": jnp.clip(0.5 * jax.random.uniform(key_list[0], (REALIZATIONS, NVAR), jnp.float32) ** steps_of(key_list[0], (REALIZATIONS, NVAR), ((1, 32),), -0.2, 0.2), 0.0, 0.5),
        "dual": jnp.clip(1.0 * jax.random.uniform(key_list[1], (REALIZATIONS, NCON), jnp.float32) ** steps_of(key_list[1], (REALIZATIONS, NCON), ((1, 32),), -0.2, 0.2), 0.0, 1.0),
        "cost": normal_values(key_list[2], (REALIZATIONS, NVAR), 1.0, 6.0, ((1, 32),), jnp.float32),
        "upper": jnp.clip(0.25 + 1.25 * jax.random.uniform(key_list[3], (NVAR,), jnp.float32) ** steps_of(key_list[3], (NVAR,), ((0, 32),), -0.2, 0.2), 0.25, 1.5),
        "rhs": normal_values(key_list[4], (NCON,), 1.0, 6.0, ((0, 32),), jnp.float32),
        "row_kind": set_ends((jax.random.randint(key_list[5], (NCON,), 0, 4) < 3).astype(jnp.int32), jax.random.fold_in(key_list[5], 1), 0, 1),
        "tiles": normal_values(key_list[6], (N_ROW * N_COL * TILES_DEV, 128, 128), (N_COL * TILES_DEV * 80 // ROWT) ** -0.5, 0.25, ((0, 32),)),
        "tile_rows": draw_tile_rows(jax.random.fold_in(key_list[10], 71), 0),
        "tile_cols": draw_tile_cols(jax.random.fold_in(key_list[10], 71), 0),
        "tile_count": draw_tile_count(jax.random.fold_in(key_list[10], 71), 0),
    }


PRIMAL_STEP = 0.4
DUAL_STEP = 0.4


def reference(primal, dual, cost, upper, rhs, row_kind, tiles, tile_rows, tile_cols, tile_count):
    width = primal.shape[0]
    row_span = ROWT * 128
    col_span = COLT * 128
    devcount = N_ROW * N_COL
    tile_sets = tiles.reshape(devcount, TILES_DEV, 128, 128)
    row_sets = tile_rows.reshape(devcount, TILES_DEV)
    col_sets = tile_cols.reshape(devcount, TILES_DEV)
    slot_ids = jnp.arange(TILES_DEV, dtype=jnp.int32)
    live_sets = (slot_ids[None, :] < tile_count[:, None]).astype(jnp.float32)
    device_ids = jnp.arange(devcount, dtype=jnp.int32)
    row_ids = jnp.arange(ROWT, dtype=jnp.int32)
    col_ids = jnp.arange(COLT, dtype=jnp.int32)

    def forward(vector):
        def visit(total, item):
            device, block, rows_here, cols_here, live_here = item
            i_row = (device // N_COL).astype(jnp.int32)
            j_col = (device % N_COL).astype(jnp.int32)
            source = lax.dynamic_slice_in_dim(vector, j_col * col_span, col_span, 1)
            pieces = source.reshape(width, COLT, 128)[:, cols_here].astype(jnp.float32)
            contrib = jnp.einsum('rtk,tjk->rtj', pieces, block.astype(jnp.float32), precision=lax.Precision.HIGHEST)
            onehot = (rows_here[:, None] == row_ids[None, :]).astype(jnp.float32) * live_here[:, None]
            part = jnp.einsum('rtj,ts->rsj', contrib, onehot, precision=lax.Precision.HIGHEST).reshape(width, row_span)
            start = i_row * row_span
            current = lax.dynamic_slice_in_dim(total, start, row_span, 1)
            return lax.dynamic_update_slice_in_dim(total, current + part, start, 1), None
        total = jnp.zeros((width, NCON), jnp.float32)
        total, _ = lax.scan(visit, total, (device_ids, tile_sets, row_sets, col_sets, live_sets))
        return total

    def adjoint(vector):
        def visit(total, item):
            device, block, rows_here, cols_here, live_here = item
            i_row = (device // N_COL).astype(jnp.int32)
            j_col = (device % N_COL).astype(jnp.int32)
            source = lax.dynamic_slice_in_dim(vector, i_row * row_span, row_span, 1)
            pieces = source.reshape(width, ROWT, 128)[:, rows_here].astype(jnp.float32)
            contrib = jnp.einsum('rtj,tjk->rtk', pieces, block.astype(jnp.float32), precision=lax.Precision.HIGHEST)
            onehot = (cols_here[:, None] == col_ids[None, :]).astype(jnp.float32) * live_here[:, None]
            part = jnp.einsum('rtk,ts->rsk', contrib, onehot, precision=lax.Precision.HIGHEST).reshape(width, col_span)
            start = j_col * col_span
            current = lax.dynamic_slice_in_dim(total, start, col_span, 1)
            return lax.dynamic_update_slice_in_dim(total, current + part, start, 1), None
        total = jnp.zeros((width, NVAR), jnp.float32)
        total, _ = lax.scan(visit, total, (device_ids, tile_sets, row_sets, col_sets, live_sets))
        return total

    state_x = primal
    state_y = dual
    for step in range(ITERS):
        grad_part = adjoint(state_y.astype(jnp.bfloat16))
        x_new = jnp.clip(state_x - PRIMAL_STEP * (cost - grad_part), 0.0, upper[None, :])
        xbar = (2.0 * x_new - state_x).astype(jnp.bfloat16)
        image = forward(xbar)
        y_new = state_y + DUAL_STEP * (rhs[None, :] - image)
        y_new = jnp.where(row_kind[None, :] == 1, jnp.maximum(y_new, 0.0), y_new)
        state_x = x_new
        state_y = y_new
    return state_x, state_y
```

```python
import functools

import jax
import jax.numpy as jnp
from jax import lax
from jax.experimental import pallas as pl
from jax.experimental.pallas import tpu as pltpu
from jax.sharding import PartitionSpec as P

ITERS = 2
PRIMAL_STEP = 0.4
DUAL_STEP = 0.4
BF16 = jnp.bfloat16
F32 = jnp.float32


def kernel(
    n_row, n_col,
    primal_h, dual_h, cost_h, upper_h, rhs_h, kind_h, tiles_h, rows_h, cols_h, count_s, rows_s, cols_s,
    out_x_h, out_y_h,
    x_v, y_v, cost_v, upper_v, rhs_v, kind_v, tiles_v, rows_v, cols_v,
    spread_g, spread_h, contrib,
    y_send, y_recv, y_full, x_send, x_recv, x_full,
    g_send, g_recv, h_send, h_recv,
    in_sem, out_sem, ys_sem, yr_sem, gs_sem, gr_sem, xs_sem, xr_sem, hs_sem, hr_sem,
):
    me_i = lax.axis_index("row")
    me_j = lax.axis_index("col")
    slots = tiles_v.shape[0]
    x_tiles = x_v.shape[1] // 128
    y_tiles = y_v.shape[1] // 128
    x_rows, y_rows = x_tiles * 8, y_tiles * 8

    barrier = pltpu.get_barrier_semaphore()
    for d in range(1, n_col):
        pl.semaphore_signal(barrier, inc=1, device_id={"col": lax.rem(me_j + d, n_col)}, device_id_type=pl.DeviceIdType.MESH)
    for d in range(1, n_row):
        pl.semaphore_signal(barrier, inc=1, device_id={"row": lax.rem(me_i + d, n_row)}, device_id_type=pl.DeviceIdType.MESH)

    loads = [
        pltpu.make_async_copy(src, dst, in_sem.at[k])
        for k, (src, dst) in enumerate((
            (dual_h, y_v), (cols_h, cols_v), (rows_h, rows_v), (tiles_h, tiles_v), (primal_h, x_v),
            (cost_h, cost_v), (upper_h, upper_v), (rhs_h, rhs_v), (kind_h, kind_v),
        ))
    ]
    for load in loads:
        load.start()
    load_dual, load_cols, load_rows, load_tiles = loads[:4]
    load_rest = loads[4:]

    sends = []

    def push(src, dst, send_sem, recv_sem, device):
        copy = pltpu.make_async_remote_copy(
            src_ref=src, dst_ref=dst, send_sem=send_sem, recv_sem=recv_sem,
            device_id=device, device_id_type=pl.DeviceIdType.MESH,
        )
        copy.start()
        sends.append(copy)

    def gather_start(it, value, tiles, send, recv, full, me, n, axis, s_sem, r_sem):
        rows = tiles * 8
        for t in range(0, tiles, 2):
            pair = jnp.concatenate([value(t), value(t + 1)], axis=0).astype(BF16)
            send[it, t * 8:(t + 2) * 8, :] = pair
            wide = pair.astype(F32)
            full[it, me * tiles + t] = wide[:8]
            full[it, me * tiles + t + 1] = wide[8:]
        for d in range(1, n):
            push(
                send.at[it], recv.at[it, pl.ds(pl.multiple_of(me * rows, 16), rows), :],
                s_sem.at[it, d - 1], r_sem.at[it, d - 1], {axis: lax.rem(me + d, n)},
            )

    def gather_wait(it, tiles, send, recv, full, me, n, axis, s_sem, r_sem):
        rows = tiles * 8
        for d in range(1, n):
            src = lax.rem(me + n - d, n)
            place = recv.at[it, pl.ds(pl.multiple_of(src * rows, 16), rows), :]
            pltpu.make_async_remote_copy(
                src_ref=send.at[it], dst_ref=place, send_sem=s_sem.at[it, d - 1], recv_sem=r_sem.at[it, d - 1],
                device_id={axis: src}, device_id_type=pl.DeviceIdType.MESH,
            ).wait_recv()
            full[it, pl.ds(src * tiles, tiles)] = place[...].astype(F32).reshape(tiles, 8, 128)

    def products(it, full, index, contract):
        for s in range(0, slots, 2):
            parts = []
            for k in (s, s + 1):
                piece = full[it, index[k]].astype(BF16)
                parts.append(lax.dot_general(
                    piece, tiles_v[k], (((1,), (contract,)), ((), ())), preferred_element_type=F32,
                ))
            both = jnp.concatenate(parts, axis=0)
            high = both.astype(BF16)
            contrib[s * 8:(s + 2) * 8, :128] = high
            contrib[s * 8:(s + 2) * 8, 128:] = (both - high.astype(F32)).astype(BF16)

    def spread(matrix, block, rows):
        part = matrix[pl.ds(pl.multiple_of(block * rows, 16), rows), :]
        total = jnp.dot(part, contrib[...], preferred_element_type=F32)
        return total[:, :128] + total[:, 128:]

    def scatter_sum(it, matrix, rows, send, recv, me, n, axis, s_sem, r_sem):
        for d in range(1, n):
            target = lax.rem(me + d, n)
            send[it, d - 1] = spread(matrix, target, rows)
            push(send.at[it, d - 1], recv.at[it, d - 1], s_sem.at[it, d - 1], r_sem.at[it, d - 1], {axis: target})
        total = spread(matrix, me, rows)
        for d in range(1, n):
            pltpu.make_async_remote_copy(
                src_ref=send.at[it, d - 1], dst_ref=recv.at[it, d - 1], send_sem=s_sem.at[it, d - 1],
                recv_sem=r_sem.at[it, d - 1], device_id={axis: lax.rem(me + d, n)},
                device_id_type=pl.DeviceIdType.MESH,
            ).wait_recv()
            total = total + recv[it, d - 1]
        return total

    lanes = slots * 8

    def build(index_v, matrix):
        slot = lax.broadcasted_iota(jnp.int32, (8, slots), 1)
        place = jnp.where(slot < count_s[0], jnp.broadcast_to(index_v[...], (8, slots)), -1)
        lane = lax.broadcasted_iota(jnp.int32, (slots, lanes), 1)
        wider = (lane // 8 == lax.broadcasted_iota(jnp.int32, (slots, lanes), 0)).astype(F32).astype(BF16)
        place = jnp.dot(place.astype(F32).astype(BF16), wider, preferred_element_type=F32)
        own = lax.broadcasted_iota(jnp.int32, (8, lanes), 1) % 8 == lax.broadcasted_iota(jnp.int32, (8, lanes), 0)
        place = jnp.where(own, place, -1.0).astype(jnp.int32)
        two = jnp.concatenate([place, place - 1], axis=0)

        def step(c, carry):
            matrix[pl.ds(pl.multiple_of(c * 16, 16), 16), :] = jnp.where(two == 2 * c, 1.0, 0.0).astype(BF16)
            return carry

        lax.fori_loop(0, matrix.shape[0] // 16, step, 0)

    load_dual.wait()
    pl.semaphore_wait(barrier, n_row + n_col - 2)
    for it in range(ITERS):
        last = it == ITERS - 1
        y_args = (y_tiles, y_send, y_recv, y_full, me_j, n_col, "col", ys_sem, yr_sem)
        gather_start(it, lambda t: y_v[:, t * 128:(t + 1) * 128], *y_args)
        if it == 0:
            load_cols.wait()
            load_rows.wait()
            build(cols_v, spread_g)
            build(rows_v, spread_h)
            load_tiles.wait()
            for load in load_rest:
                load.wait()
        gather_wait(it, *y_args)
        products(it, y_full, rows_s, 0)
        grad = scatter_sum(it, spread_g, x_rows, g_send, g_recv, me_i, n_row, "row", gs_sem, gr_sem)
        bars = []
        for t in range(x_tiles):
            cut = slice(t * 128, (t + 1) * 128)
            x = x_v[:, cut]
            moved = x - PRIMAL_STEP * (cost_v[:, cut] - grad[t * 8:(t + 1) * 8])
            x_new = jnp.minimum(jnp.maximum(moved, 0.0), upper_v[:, cut])
            bars.append(2.0 * x_new - x)
            x_v[:, cut] = x_new
        x_args = (x_tiles, x_send, x_recv, x_full, me_i, n_row, "row", xs_sem, xr_sem)
        gather_start(it, lambda t: bars[t], *x_args)
        if last:
            store_x = pltpu.make_async_copy(x_v, out_x_h, out_sem.at[0])
            store_x.start()
        gather_wait(it, *x_args)
        products(it, x_full, cols_s, 1)
        image = scatter_sum(it, spread_h, y_rows, h_send, h_recv, me_j, n_col, "col", hs_sem, hr_sem)
        for t in range(y_tiles):
            cut = slice(t * 128, (t + 1) * 128)
            y_new = y_v[:, cut] + DUAL_STEP * (rhs_v[:, cut] - image[t * 8:(t + 1) * 8])
            y_v[:, cut] = jnp.where(kind_v[:, cut] == 1, jnp.maximum(y_new, 0.0), y_new)
    store_y = pltpu.make_async_copy(y_v, out_y_h, out_sem.at[1])
    store_y.start()
    for copy in sends:
        copy.wait_send()
    store_x.wait()
    store_y.wait()


def body(primal, dual, cost, upper, rhs, row_kind, tiles, tile_rows, tile_cols, tile_count):
    n_row = lax.axis_size("row")
    n_col = lax.axis_size("col")
    x_width, y_width = primal.shape[1], dual.shape[1]
    slots = tiles.shape[0]
    x_rows, y_rows = x_width // 16, y_width // 16
    g_rows, h_rows = x_rows * n_row, y_rows * n_col
    any_spec = pl.BlockSpec(memory_space=pl.ANY)
    smem_spec = pl.BlockSpec(memory_space=pltpu.SMEM)
    dma = pltpu.SemaphoreType.DMA
    scratch = [
        pltpu.VMEM((8, x_width), F32), pltpu.VMEM((8, y_width), F32), pltpu.VMEM((8, x_width), F32),
        pltpu.VMEM((1, x_width), F32), pltpu.VMEM((1, y_width), F32), pltpu.VMEM((1, y_width), jnp.int32),
        pltpu.VMEM(tiles.shape, BF16), pltpu.VMEM((1, slots), jnp.int32), pltpu.VMEM((1, slots), jnp.int32),
        pltpu.VMEM((g_rows, slots * 8), BF16), pltpu.VMEM((h_rows, slots * 8), BF16),
        pltpu.VMEM((slots * 8, 256), BF16),
        pltpu.VMEM((ITERS, y_rows, 128), BF16), pltpu.VMEM((ITERS, h_rows, 128), BF16),
        pltpu.VMEM((ITERS, h_rows // 8, 8, 128), F32),
        pltpu.VMEM((ITERS, x_rows, 128), BF16), pltpu.VMEM((ITERS, g_rows, 128), BF16),
        pltpu.VMEM((ITERS, g_rows // 8, 8, 128), F32),
        pltpu.VMEM((ITERS, n_row - 1, x_rows, 128), F32), pltpu.VMEM((ITERS, n_row - 1, x_rows, 128), F32),
        pltpu.VMEM((ITERS, n_col - 1, y_rows, 128), F32), pltpu.VMEM((ITERS, n_col - 1, y_rows, 128), F32),
        dma((9,)), dma((2,)),
        dma((ITERS, n_col - 1)), dma((ITERS, n_col - 1)), dma((ITERS, n_row - 1)), dma((ITERS, n_row - 1)),
        dma((ITERS, n_row - 1)), dma((ITERS, n_row - 1)), dma((ITERS, n_col - 1)), dma((ITERS, n_col - 1)),
    ]
    return pl.pallas_call(
        functools.partial(kernel, n_row, n_col),
        out_shape=(jax.ShapeDtypeStruct(primal.shape, F32), jax.ShapeDtypeStruct(dual.shape, F32)),
        in_specs=[any_spec] * 9 + [smem_spec] * 3,
        out_specs=(any_spec, any_spec),
        scratch_shapes=scratch,
        compiler_params=pltpu.CompilerParams(
            collective_id=0, has_side_effects=True, vmem_limit_bytes=40 * 1024 * 1024,
        ),
        name="pdhg",
    )(
        primal, dual, cost, upper.reshape(1, -1), rhs.reshape(1, -1), row_kind.reshape(1, -1), tiles,
        tile_rows.reshape(1, -1), tile_cols.reshape(1, -1), tile_count, tile_rows, tile_cols,
    )


def solution(mesh):
    in_specs = (
        P(None, ("col", "row")),
        P(None, ("row", "col")),
        P(None, ("col", "row")),
        P(("col", "row")),
        P(("row", "col")),
        P(("row", "col")),
        P(("row", "col"), None, None),
        P(("row", "col")),
        P(("row", "col")),
        P(("row", "col")),
    )
    out_specs = (P(None, ("col", "row")), P(None, ("row", "col")))
    return jax.shard_map(body, mesh=mesh, in_specs=in_specs, out_specs=out_specs, check_vma=False)
```

```python
import functools

import jax
import jax.numpy as jnp
from jax import lax
from jax.experimental import pallas as pl
from jax.experimental.pallas import tpu as pltpu
from jax.sharding import PartitionSpec as P

ITERS = 2
PRIMAL_STEP = 0.4
DUAL_STEP = 0.4
BF16 = jnp.bfloat16
F32 = jnp.float32


def kernel(
    n_row, n_col,
    primal_h, dual_h, cost_h, upper_h, rhs_h, kind_h, tiles_h, rows_h, cols_h, count_s, rows_s, cols_s,
    out_x_h, out_y_h,
    x_v, y_v, cost_v, upper_v, rhs_v, kind_v, tiles_v, rows_v, cols_v,
    spread_g, spread_h, contrib,
    y_send, y_recv, y_full, x_send, x_recv, x_full,
    g_send, g_recv, h_send, h_recv,
    in_sem, out_sem, ys_sem, yr_sem, gs_sem, gr_sem, xs_sem, xr_sem, hs_sem, hr_sem,
):
    me_i = lax.axis_index("row")
    me_j = lax.axis_index("col")
    slots = tiles_v.shape[0]
    x_tiles = x_v.shape[1] // 128
    y_tiles = y_v.shape[1] // 128
    x_rows, y_rows = x_tiles * 8, y_tiles * 8

    barrier = pltpu.get_barrier_semaphore()
    for d in range(1, n_col):
        pl.semaphore_signal(barrier, inc=1, device_id={"col": lax.rem(me_j + d, n_col)}, device_id_type=pl.DeviceIdType.MESH)
    for d in range(1, n_row):
        pl.semaphore_signal(barrier, inc=1, device_id={"row": lax.rem(me_i + d, n_row)}, device_id_type=pl.DeviceIdType.MESH)

    loads = [
        pltpu.make_async_copy(src, dst, in_sem.at[k])
        for k, (src, dst) in enumerate((
            (dual_h, y_v), (cols_h, cols_v), (rows_h, rows_v), (tiles_h, tiles_v), (primal_h, x_v),
            (cost_h, cost_v), (upper_h, upper_v), (rhs_h, rhs_v), (kind_h, kind_v),
        ))
    ]
    for load in loads:
        load.start()
    load_dual, load_cols, load_rows, load_tiles = loads[:4]
    load_rest = loads[4:]

    sends = []

    def push(src, dst, send_sem, recv_sem, device):
        copy = pltpu.make_async_remote_copy(
            src_ref=src, dst_ref=dst, send_sem=send_sem, recv_sem=recv_sem,
            device_id=device, device_id_type=pl.DeviceIdType.MESH,
        )
        copy.start()
        sends.append(copy)

    def gather_start(it, value, tiles, send, recv, full, me, n, axis, s_sem, r_sem):
        rows = tiles * 8
        for t in range(0, tiles, 2):
            pair = jnp.concatenate([value(t), value(t + 1)], axis=0).astype(BF16)
            send[it, t * 8:(t + 2) * 8, :] = pair
            wide = pair.astype(F32)
            full[it, me * tiles + t] = wide[:8]
            full[it, me * tiles + t + 1] = wide[8:]
        for d in range(1, n):
            push(
                send.at[it], recv.at[it, pl.ds(pl.multiple_of(me * rows, 16), rows), :],
                s_sem.at[it, d - 1], r_sem.at[it, d - 1], {axis: lax.rem(me + d, n)},
            )

    def gather_wait(it, tiles, send, recv, full, me, n, axis, s_sem, r_sem):
        rows = tiles * 8
        for d in range(1, n):
            src = lax.rem(me + n - d, n)
            place = recv.at[it, pl.ds(pl.multiple_of(src * rows, 16), rows), :]
            pltpu.make_async_remote_copy(
                src_ref=send.at[it], dst_ref=place, send_sem=s_sem.at[it, d - 1], recv_sem=r_sem.at[it, d - 1],
                device_id={axis: src}, device_id_type=pl.DeviceIdType.MESH,
            ).wait_recv()
            full[it, pl.ds(src * tiles, tiles)] = place[...].astype(F32).reshape(tiles, 8, 128)

    def products(it, full, index, contract):
        for s in range(0, slots, 2):
            parts = []
            for k in (s, s + 1):
                piece = full[it, index[k]].astype(BF16)
                parts.append(lax.dot_general(
                    piece, tiles_v[k], (((1,), (contract,)), ((), ())), preferred_element_type=F32,
                ))
            both = jnp.concatenate(parts, axis=0)
            high = both.astype(BF16)
            contrib[s * 8:(s + 2) * 8, :128] = high
            contrib[s * 8:(s + 2) * 8, 128:] = (both - high.astype(F32)).astype(BF16)

    def scatter_sum(it, matrix, rows, send, recv, me, n, axis, s_sem, r_sem):
        whole = jnp.dot(matrix[...], contrib[...], preferred_element_type=F32)
        send[it] = whole[:, :128] + whole[:, 128:]

        def block(index):
            return send.at[it, pl.ds(pl.multiple_of(index * rows, 16), rows), :]

        for d in range(1, n):
            target = lax.rem(me + d, n)
            push(block(target), recv.at[it, d - 1], s_sem.at[it, d - 1], r_sem.at[it, d - 1], {axis: target})
        total = block(me)[...]
        for d in range(1, n):
            source = lax.rem(me + n - d, n)
            pltpu.make_async_remote_copy(
                src_ref=block(source), dst_ref=recv.at[it, d - 1], send_sem=s_sem.at[it, d - 1],
                recv_sem=r_sem.at[it, d - 1], device_id={axis: source}, device_id_type=pl.DeviceIdType.MESH,
            ).wait_recv()
            total = total + recv[it, d - 1]
        return total

    lanes = slots * 8

    def build(index_v, matrix):
        slot = lax.broadcasted_iota(jnp.int32, (8, slots), 1)
        place = jnp.where(slot < count_s[0], jnp.broadcast_to(index_v[...], (8, slots)), -1)
        lane = lax.broadcasted_iota(jnp.int32, (slots, lanes), 1)
        wider = (lane // 8 == lax.broadcasted_iota(jnp.int32, (slots, lanes), 0)).astype(F32).astype(BF16)
        place = jnp.dot(place.astype(F32).astype(BF16), wider, preferred_element_type=F32)
        own = lax.broadcasted_iota(jnp.int32, (8, lanes), 1) % 8 == lax.broadcasted_iota(jnp.int32, (8, lanes), 0)
        place = jnp.where(own, place, -1.0).astype(jnp.int32)
        two = jnp.concatenate([place, place - 1], axis=0)

        def step(c, carry):
            matrix[pl.ds(pl.multiple_of(c * 16, 16), 16), :] = jnp.where(two == 2 * c, 1.0, 0.0).astype(BF16)
            return carry

        lax.fori_loop(0, matrix.shape[0] // 16, step, 0)

    load_dual.wait()
    pl.semaphore_wait(barrier, n_row + n_col - 2)
    for it in range(ITERS):
        last = it == ITERS - 1
        y_args = (y_tiles, y_send, y_recv, y_full, me_j, n_col, "col", ys_sem, yr_sem)
        gather_start(it, lambda t: y_v[:, t * 128:(t + 1) * 128], *y_args)
        if it == 0:
            load_cols.wait()
            load_rows.wait()
            build(cols_v, spread_g)
            build(rows_v, spread_h)
            load_tiles.wait()
            for load in load_rest:
                load.wait()
        gather_wait(it, *y_args)
        products(it, y_full, rows_s, 0)
        grad = scatter_sum(it, spread_g, x_rows, g_send, g_recv, me_i, n_row, "row", gs_sem, gr_sem)
        bars = []
        for t in range(x_tiles):
            cut = slice(t * 128, (t + 1) * 128)
            x = x_v[:, cut]
            moved = x - PRIMAL_STEP * (cost_v[:, cut] - grad[t * 8:(t + 1) * 8])
            x_new = jnp.minimum(jnp.maximum(moved, 0.0), upper_v[:, cut])
            bars.append(2.0 * x_new - x)
            x_v[:, cut] = x_new
        x_args = (x_tiles, x_send, x_recv, x_full, me_i, n_row, "row", xs_sem, xr_sem)
        gather_start(it, lambda t: bars[t], *x_args)
        if last:
            store_x = pltpu.make_async_copy(x_v, out_x_h, out_sem.at[0])
            store_x.start()
        gather_wait(it, *x_args)
        products(it, x_full, cols_s, 1)
        image = scatter_sum(it, spread_h, y_rows, h_send, h_recv, me_j, n_col, "col", hs_sem, hr_sem)
        for t in range(y_tiles):
            cut = slice(t * 128, (t + 1) * 128)
            y_new = y_v[:, cut] + DUAL_STEP * (rhs_v[:, cut] - image[t * 8:(t + 1) * 8])
            y_v[:, cut] = jnp.where(kind_v[:, cut] == 1, jnp.maximum(y_new, 0.0), y_new)
    store_y = pltpu.make_async_copy(y_v, out_y_h, out_sem.at[1])
    store_y.start()
    for copy in sends:
        copy.wait_send()
    store_x.wait()
    store_y.wait()


def body(primal, dual, cost, upper, rhs, row_kind, tiles, tile_rows, tile_cols, tile_count):
    n_row = lax.axis_size("row")
    n_col = lax.axis_size("col")
    x_width, y_width = primal.shape[1], dual.shape[1]
    slots = tiles.shape[0]
    x_rows, y_rows = x_width // 16, y_width // 16
    g_rows, h_rows = x_rows * n_row, y_rows * n_col
    any_spec = pl.BlockSpec(memory_space=pl.ANY)
    smem_spec = pl.BlockSpec(memory_space=pltpu.SMEM)
    dma = pltpu.SemaphoreType.DMA
    scratch = [
        pltpu.VMEM((8, x_width), F32), pltpu.VMEM((8, y_width), F32), pltpu.VMEM((8, x_width), F32),
        pltpu.VMEM((1, x_width), F32), pltpu.VMEM((1, y_width), F32), pltpu.VMEM((1, y_width), jnp.int32),
        pltpu.VMEM(tiles.shape, BF16), pltpu.VMEM((1, slots), jnp.int32), pltpu.VMEM((1, slots), jnp.int32),
        pltpu.VMEM((g_rows, slots * 8), BF16), pltpu.VMEM((h_rows, slots * 8), BF16),
        pltpu.VMEM((slots * 8, 256), BF16),
        pltpu.VMEM((ITERS, y_rows, 128), BF16), pltpu.VMEM((ITERS, h_rows, 128), BF16),
        pltpu.VMEM((ITERS, h_rows // 8, 8, 128), F32),
        pltpu.VMEM((ITERS, x_rows, 128), BF16), pltpu.VMEM((ITERS, g_rows, 128), BF16),
        pltpu.VMEM((ITERS, g_rows // 8, 8, 128), F32),
        pltpu.VMEM((ITERS, g_rows, 128), F32), pltpu.VMEM((ITERS, n_row - 1, x_rows, 128), F32),
        pltpu.VMEM((ITERS, h_rows, 128), F32), pltpu.VMEM((ITERS, n_col - 1, y_rows, 128), F32),
        dma((9,)), dma((2,)),
        dma((ITERS, n_col - 1)), dma((ITERS, n_col - 1)), dma((ITERS, n_row - 1)), dma((ITERS, n_row - 1)),
        dma((ITERS, n_row - 1)), dma((ITERS, n_row - 1)), dma((ITERS, n_col - 1)), dma((ITERS, n_col - 1)),
    ]
    return pl.pallas_call(
        functools.partial(kernel, n_row, n_col),
        out_shape=(jax.ShapeDtypeStruct(primal.shape, F32), jax.ShapeDtypeStruct(dual.shape, F32)),
        in_specs=[any_spec] * 9 + [smem_spec] * 3,
        out_specs=(any_spec, any_spec),
        scratch_shapes=scratch,
        compiler_params=pltpu.CompilerParams(
            collective_id=0, has_side_effects=True, vmem_limit_bytes=60 * 1024 * 1024,
        ),
        name="pdhg",
    )(
        primal, dual, cost, upper.reshape(1, -1), rhs.reshape(1, -1), row_kind.reshape(1, -1), tiles,
        tile_rows.reshape(1, -1), tile_cols.reshape(1, -1), tile_count, tile_rows, tile_cols,
    )


def solution(mesh):
    in_specs = (
        P(None, ("col", "row")),
        P(None, ("row", "col")),
        P(None, ("col", "row")),
        P(("col", "row")),
        P(("row", "col")),
        P(("row", "col")),
        P(("row", "col"), None, None),
        P(("row", "col")),
        P(("row", "col")),
        P(("row", "col")),
    )
    out_specs = (P(None, ("col", "row")), P(None, ("row", "col")))
    return jax.shard_map(body, mesh=mesh, in_specs=in_specs, out_specs=out_specs, check_vma=False)
```

```python
import functools

import jax
import jax.numpy as jnp
from jax import lax
from jax.experimental import pallas as pl
from jax.experimental.pallas import tpu as pltpu
from jax.sharding import PartitionSpec as P

ITERS = 2
GROUPS = 2
HALF = 4
PRIMAL_STEP = 0.4
DUAL_STEP = 0.4
BF16 = jnp.bfloat16
F32 = jnp.float32


def kernel(
    n_row, n_col,
    primal_h, dual_h, cost_h, upper_h, rhs_h, kind_h, tiles_h, rows_h, cols_h, count_s, rows_s, cols_s,
    out_x_h, out_y_h,
    x_v, y_v, cost_v, upper_v, rhs_v, kind_v, tiles_v, rows_v, cols_v,
    x_st, y_st, cost_st, upper_st, rhs_st, kind_st,
    spread_g, spread_h, contrib,
    y_send, y_recv, y_full, x_send, x_recv, x_full,
    g_send, g_recv, h_send, h_recv,
    in_sem, out_sem, ys_sem, yr_sem, gs_sem, gr_sem, xs_sem, xr_sem, hs_sem, hr_sem,
):
    me_i = lax.axis_index("row")
    me_j = lax.axis_index("col")
    slots = tiles_v.shape[0]
    x_tiles = x_v.shape[1] // 128
    y_tiles = y_v.shape[1] // 128

    barrier = pltpu.get_barrier_semaphore()
    for d in range(1, n_col):
        pl.semaphore_signal(barrier, inc=1, device_id={"col": lax.rem(me_j + d, n_col)}, device_id_type=pl.DeviceIdType.MESH)
    for d in range(1, n_row):
        pl.semaphore_signal(barrier, inc=1, device_id={"row": lax.rem(me_i + d, n_row)}, device_id_type=pl.DeviceIdType.MESH)

    loads = [
        pltpu.make_async_copy(src, dst, in_sem.at[k])
        for k, (src, dst) in enumerate((
            (dual_h, y_v), (cols_h, cols_v), (rows_h, rows_v), (tiles_h, tiles_v), (primal_h, x_v),
            (cost_h, cost_v), (upper_h, upper_v), (rhs_h, rhs_v), (kind_h, kind_v),
        ))
    ]
    for load in loads:
        load.start()

    def to_rows(ref, group, tiles):
        return jnp.concatenate(
            [ref[group * HALF:(group + 1) * HALF, t * 128:(t + 1) * 128] for t in range(tiles)], axis=0
        )

    def spread_rows(ref, tiles):
        return jnp.concatenate(
            [jnp.broadcast_to(ref[:, t * 128:(t + 1) * 128], (HALF, 128)) for t in range(tiles)], axis=0
        )

    def from_rows(ref, group, value, tiles):
        for t in range(tiles):
            ref[group * HALF:(group + 1) * HALF, t * 128:(t + 1) * 128] = value[t * HALF:(t + 1) * HALF]

    def push(src, dst, send_sem, recv_sem, device):
        pltpu.make_async_remote_copy(
            src_ref=src, dst_ref=dst, send_sem=send_sem, recv_sem=recv_sem,
            device_id=device, device_id_type=pl.DeviceIdType.MESH,
        ).start()

    def drain(recv, sem, it, group):
        whole = recv.at[it, group]
        pltpu.make_async_copy(whole, whole, sem.at[it, group]).wait()

    def fill(full, it, group, first, value, tiles):
        for t in range(tiles):
            part = value[t * HALF:(t + 1) * HALF]
            full[it, group, first + t] = jnp.concatenate([part, part], axis=0)

    def gather_start(it, group, value, tiles, send, recv, full, me, n, axis, s_sem, r_sem):
        low = value.astype(BF16)
        send[it, group] = low
        for d in range(1, n):
            push(
                send.at[it, group], recv.at[it, group, d - 1], s_sem.at[it, group], r_sem.at[it, group],
                {axis: lax.rem(me + d, n)},
            )
        fill(full, it, group, me * tiles, low.astype(F32), tiles)

    def gather_wait(it, group, tiles, send, recv, full, me, n, axis, s_sem, r_sem):
        drain(recv, r_sem, it, group)
        for d in range(1, n):
            source = lax.rem(me + n - d, n)
            fill(full, it, group, source * tiles, recv[it, group, d - 1].astype(F32), tiles)

    upper_half = lax.broadcasted_iota(jnp.int32, (8, 128), 0) < HALF

    def products(it, group, full, index, forward):
        for s in range(0, slots, 2):
            one = jnp.where(upper_half, full[it, group, index[s]], 0.0)
            two = jnp.where(upper_half, 0.0, full[it, group, index[s + 1]])
            left = jnp.concatenate([one, two], axis=1).astype(BF16)
            if forward:
                right = jnp.concatenate([tiles_v[s], tiles_v[s + 1]], axis=1)
                both = lax.dot_general(left, right, (((1,), (1,)), ((), ())), preferred_element_type=F32)
            else:
                right = tiles_v[s:s + 2].reshape(256, 128)
                both = jnp.dot(left, right, preferred_element_type=F32)
            contrib[group, s * HALF:(s + 2) * HALF, :] = both

    def scatter_start(it, group, matrix, rows, send, recv, me, n, axis, s_sem, r_sem):
        terms = contrib[group]
        high = terms.astype(BF16)
        rest = (terms - high.astype(F32)).astype(BF16)
        whole = jnp.dot(matrix[...], jnp.concatenate([high, rest], axis=1), preferred_element_type=F32)
        send[it, group] = (whole[:, :128] + whole[:, 128:]).reshape(n, rows, 128)
        for d in range(1, n):
            target = lax.rem(me + d, n)
            push(
                send.at[it, group, target], recv.at[it, group, d - 1], s_sem.at[it, group], r_sem.at[it, group],
                {axis: target},
            )

    def scatter_wait(it, group, matrix, rows, send, recv, me, n, axis, s_sem, r_sem):
        drain(recv, r_sem, it, group)
        total = send[it, group, me]
        for d in range(1, n):
            total = total + recv[it, group, d - 1]
        return total

    lanes = slots * HALF

    def build(index_v, matrix):
        slot = lax.broadcasted_iota(jnp.int32, (8, slots), 1)
        place = jnp.where(slot < count_s[0], jnp.broadcast_to(index_v[...], (8, slots)), -1)
        lane = lax.broadcasted_iota(jnp.int32, (slots, lanes), 1)
        wider = (lane // HALF == lax.broadcasted_iota(jnp.int32, (slots, lanes), 0)).astype(F32).astype(BF16)
        place = jnp.dot(place.astype(F32).astype(BF16), wider, preferred_element_type=F32)
        sub = lax.broadcasted_iota(jnp.int32, (8, lanes), 0)
        own = lax.broadcasted_iota(jnp.int32, (8, lanes), 1) % HALF == sub % HALF
        place = jnp.where(own, place, -100000.0).astype(jnp.int32) - sub // HALF
        two = jnp.concatenate([place, place - 2], axis=0)

        def step(c, carry):
            matrix[pl.ds(pl.multiple_of(c * 16, 16), 16), :] = jnp.where(two == 4 * c, 1.0, 0.0).astype(BF16)
            return carry

        lax.fori_loop(0, matrix.shape[0] // 16, step, 0)

    y_args = (y_tiles, y_send, y_recv, y_full, me_j, n_col, "col", ys_sem, yr_sem)
    x_args = (x_tiles, x_send, x_recv, x_full, me_i, n_row, "row", xs_sem, xr_sem)
    g_args = (spread_g, x_tiles * HALF, g_send, g_recv, me_i, n_row, "row", gs_sem, gr_sem)
    h_args = (spread_h, y_tiles * HALF, h_send, h_recv, me_j, n_col, "col", hs_sem, hr_sem)

    loads[0].wait()
    for group in range(GROUPS):
        y_st[group] = to_rows(y_v, group, y_tiles)
    pl.semaphore_wait(barrier, n_row + n_col - 2)
    for group in range(GROUPS):
        gather_start(0, group, y_st[group], *y_args)
    for load in loads[1:]:
        load.wait()
    build(cols_v, spread_g)
    build(rows_v, spread_h)
    for group in range(GROUPS):
        x_st[group] = to_rows(x_v, group, x_tiles)
        cost_st[group] = to_rows(cost_v, group, x_tiles)
    upper_st[...] = spread_rows(upper_v, x_tiles)
    rhs_st[...] = spread_rows(rhs_v, y_tiles)
    kind_st[...] = spread_rows(kind_v, y_tiles)
    stores = (pltpu.make_async_copy(x_v, out_x_h, out_sem.at[0]), pltpu.make_async_copy(y_v, out_y_h, out_sem.at[1]))
    for it in range(ITERS):
        last = it == ITERS - 1
        for group in range(GROUPS):
            gather_wait(it, group, *y_args)
            products(it, group, y_full, rows_s, False)
            scatter_start(it, group, *g_args)
        for group in range(GROUPS):
            grad = scatter_wait(it, group, *g_args)
            x = x_st[group]
            moved = x - PRIMAL_STEP * (cost_st[group] - grad)
            x_new = jnp.minimum(jnp.maximum(moved, 0.0), upper_st[...])
            gather_start(it, group, 2.0 * x_new - x, *x_args)
            x_st[group] = x_new
            if last:
                from_rows(x_v, group, x_new, x_tiles)
        if last:
            stores[0].start()
        for group in range(GROUPS):
            gather_wait(it, group, *x_args)
            products(it, group, x_full, cols_s, True)
            scatter_start(it, group, *h_args)
        for group in range(GROUPS):
            image = scatter_wait(it, group, *h_args)
            y_new = y_st[group] + DUAL_STEP * (rhs_st[...] - image)
            y_new = jnp.where(kind_st[...] == 1, jnp.maximum(y_new, 0.0), y_new)
            if last:
                from_rows(y_v, group, y_new, y_tiles)
            else:
                y_st[group] = y_new
                gather_start(it + 1, group, y_new, *y_args)
    stores[1].start()
    for it in range(ITERS):
        for group in range(GROUPS):
            drain(y_recv, ys_sem, it, group)
            drain(g_recv, gs_sem, it, group)
            drain(x_recv, xs_sem, it, group)
            drain(h_recv, hs_sem, it, group)
    for store in stores:
        store.wait()


def hand_out(x_in, y_in, x_out, y_out, sem):
    copies = (pltpu.make_async_copy(x_in, x_out, sem.at[0]), pltpu.make_async_copy(y_in, y_out, sem.at[1]))
    for copy in copies:
        copy.start()
    for copy in copies:
        copy.wait()


def body(primal, dual, cost, upper, rhs, row_kind, tiles, tile_rows, tile_cols, tile_count):
    n_row = lax.axis_size("row")
    n_col = lax.axis_size("col")
    x_width, y_width = primal.shape[1], dual.shape[1]
    slots = tiles.shape[0]
    x_rows, y_rows = x_width // 128 * HALF, y_width // 128 * HALF
    any_spec = pl.BlockSpec(memory_space=pl.ANY)
    smem_spec = pl.BlockSpec(memory_space=pltpu.SMEM)
    dma = pltpu.SemaphoreType.DMA
    both = (ITERS, GROUPS)

    def exchange(n, rows):
        return [
            pltpu.VMEM(both + (rows, 128), BF16), pltpu.VMEM(both + (n - 1, rows, 128), BF16),
            pltpu.VMEM(both + (n * rows // HALF, 8, 128), F32),
        ]

    def partial(n, rows):
        return [pltpu.VMEM(both + (n, rows, 128), F32), pltpu.VMEM(both + (n - 1, rows, 128), F32)]

    scratch = [
        pltpu.VMEM((8, x_width), F32), pltpu.VMEM((8, y_width), F32), pltpu.VMEM((8, x_width), F32),
        pltpu.VMEM((1, x_width), F32), pltpu.VMEM((1, y_width), F32), pltpu.VMEM((1, y_width), jnp.int32),
        pltpu.VMEM(tiles.shape, BF16), pltpu.VMEM((1, slots), jnp.int32), pltpu.VMEM((1, slots), jnp.int32),
        pltpu.VMEM((GROUPS, x_rows, 128), F32), pltpu.VMEM((GROUPS, y_rows, 128), F32),
        pltpu.VMEM((GROUPS, x_rows, 128), F32), pltpu.VMEM((x_rows, 128), F32),
        pltpu.VMEM((y_rows, 128), F32), pltpu.VMEM((y_rows, 128), jnp.int32),
        pltpu.VMEM((x_rows * n_row, slots * HALF), BF16), pltpu.VMEM((y_rows * n_col, slots * HALF), BF16),
        pltpu.VMEM((GROUPS, slots * HALF, 128), F32),
    ]
    scratch += exchange(n_col, y_rows) + exchange(n_row, x_rows) + partial(n_row, x_rows) + partial(n_col, y_rows)
    scratch += [dma((9,)), dma((2,))] + [dma(both)] * 8
    results = pl.pallas_call(
        functools.partial(kernel, n_row, n_col),
        out_shape=(jax.ShapeDtypeStruct(primal.shape, F32), jax.ShapeDtypeStruct(dual.shape, F32)),
        in_specs=[any_spec] * 9 + [smem_spec] * 3,
        out_specs=(any_spec, any_spec),
        scratch_shapes=scratch,
        compiler_params=pltpu.CompilerParams(
            collective_id=0, has_side_effects=True, vmem_limit_bytes=60 * 1024 * 1024,
        ),
        name="pdhg",
    )(
        primal, dual, cost, upper.reshape(1, -1), rhs.reshape(1, -1), row_kind.reshape(1, -1), tiles,
        tile_rows.reshape(1, -1), tile_cols.reshape(1, -1), tile_count, tile_rows, tile_cols,
    )
    return pl.pallas_call(
        hand_out,
        out_shape=(jax.ShapeDtypeStruct(primal.shape, F32), jax.ShapeDtypeStruct(dual.shape, F32)),
        in_specs=[any_spec] * 2,
        out_specs=(any_spec, any_spec),
        scratch_shapes=[dma((2,))],
        compiler_params=pltpu.CompilerParams(vmem_limit_bytes=60 * 1024 * 1024),
        name="hand_out",
    )(*results)


def solution(mesh):
    in_specs = (
        P(None, ("col", "row")),
        P(None, ("row", "col")),
        P(None, ("col", "row")),
        P(("col", "row")),
        P(("row", "col")),
        P(("row", "col")),
        P(("row", "col"), None, None),
        P(("row", "col")),
        P(("row", "col")),
        P(("row", "col")),
    )
    out_specs = (P(None, ("col", "row")), P(None, ("row", "col")))
    return jax.shard_map(body, mesh=mesh, in_specs=in_specs, out_specs=out_specs, check_vma=False)
```

```python
import functools

import jax
import jax.numpy as jnp
from jax import lax
from jax.experimental import pallas as pl
from jax.experimental.pallas import tpu as pltpu
from jax.sharding import PartitionSpec as P

ITERS = 2
GROUPS = 2
HALF = 4
PRIMAL_STEP = 0.4
DUAL_STEP = 0.4
BF16 = jnp.bfloat16
F32 = jnp.float32


def kernel(
    n_row, n_col,
    primal_h, dual_h, cost_h, upper_h, rhs_h, kind_h, tiles_h, rows_h, cols_h, count_s,
    out_x_h, out_y_h,
    x_v, y_v, cost_v, upper_v, rhs_v, kind_v, tiles_v, rows_v, cols_v, rows_s, cols_s,
    x_st, y_st, cost_st, upper_st, rhs_st, kind_st,
    turned, spread_g, spread_h, contrib,
    y_send, y_recv, y_full, x_send, x_recv, x_full,
    g_send, g_recv, h_send, h_recv, low_send, low_recv,
    in_sem, out_sem, ys_sem, yr_sem, gs_sem, gr_sem, xs_sem, xr_sem, hs_sem, hr_sem,
):
    me_i = lax.axis_index("row")
    me_j = lax.axis_index("col")
    slots = tiles_v.shape[0]
    x_tiles = x_v.shape[1] // 128
    y_tiles = y_v.shape[1] // 128

    barrier = pltpu.get_barrier_semaphore()
    for d in range(1, n_col):
        pl.semaphore_signal(barrier, inc=1, device_id={"col": lax.rem(me_j + d, n_col)}, device_id_type=pl.DeviceIdType.MESH)
    for d in range(1, n_row):
        pl.semaphore_signal(barrier, inc=1, device_id={"row": lax.rem(me_i + d, n_row)}, device_id_type=pl.DeviceIdType.MESH)

    loads = [
        pltpu.make_async_copy(src, dst, in_sem.at[k])
        for k, (src, dst) in enumerate((
            (dual_h, y_v), (cols_h, cols_v), (rows_h, rows_v), (tiles_h, tiles_v), (primal_h, x_v),
            (cost_h, cost_v), (upper_h, upper_v), (rhs_h, rhs_v), (kind_h, kind_v),
            (rows_h, rows_s), (cols_h, cols_s),
        ))
    ]
    for load in loads:
        load.start()

    def to_rows(ref, group, tiles):
        return jnp.concatenate(
            [ref[group * HALF:(group + 1) * HALF, t * 128:(t + 1) * 128] for t in range(tiles)], axis=0
        )

    def spread_rows(ref, tiles):
        return jnp.concatenate(
            [jnp.broadcast_to(ref[:, t * 128:(t + 1) * 128], (HALF, 128)) for t in range(tiles)], axis=0
        )

    def from_rows(ref, group, value, tiles):
        for t in range(tiles):
            ref[group * HALF:(group + 1) * HALF, t * 128:(t + 1) * 128] = value[t * HALF:(t + 1) * HALF]

    def push(src, dst, send_sem, recv_sem, device):
        pltpu.make_async_remote_copy(
            src_ref=src, dst_ref=dst, send_sem=send_sem, recv_sem=recv_sem,
            device_id=device, device_id_type=pl.DeviceIdType.MESH,
        ).start()

    def drain(recv, sem, it, group):
        whole = recv.at[it, group]
        pltpu.make_async_copy(whole, whole, sem.at[it, group]).wait()

    def drain_low(sem, it, group):
        whole = low_recv.at[group]
        pltpu.make_async_copy(whole, whole, sem.at[it, group]).wait()

    def fill(full, it, group, first, value, tiles):
        for t in range(tiles):
            part = value[t * HALF:(t + 1) * HALF]
            full[it, group, first + t] = jnp.concatenate([part, part], axis=0)

    def gather_start(it, group, value, tiles, send, recv, full, me, n, axis, s_sem, r_sem):
        low = value.astype(BF16)
        send[it, group] = low
        for d in range(1, n):
            push(
                send.at[it, group], recv.at[it, group, d - 1], s_sem.at[it, group], r_sem.at[it, group],
                {axis: lax.rem(me + d, n)},
            )
        fill(full, it, group, me * tiles, low.astype(F32), tiles)

    def gather_wait(it, group, tiles, send, recv, full, me, n, axis, s_sem, r_sem):
        drain(recv, r_sem, it, group)
        for d in range(1, n):
            source = lax.rem(me + n - d, n)
            fill(full, it, group, source * tiles, recv[it, group, d - 1].astype(F32), tiles)

    upper_half = lax.broadcasted_iota(jnp.int32, (8, 128), 0) < HALF

    def products(it, group, full, index, blocks):
        for s in range(0, slots, 2):
            one = jnp.where(upper_half, full[it, group, index[0, s]], 0.0)
            two = jnp.where(upper_half, 0.0, full[it, group, index[0, s + 1]])
            left = jnp.concatenate([one, two], axis=1).astype(BF16)
            both = jnp.dot(left, blocks[s:s + 2].reshape(256, 128), preferred_element_type=F32)
            contrib[group, s * HALF:(s + 2) * HALF, :] = both

    def scatter_start(it, group, matrix, rows, send, recv, me, n, axis, s_sem, r_sem, narrow=False):
        terms = contrib[group]
        high = terms.astype(BF16)
        rest = (terms - high.astype(F32)).astype(BF16)
        whole = jnp.dot(matrix[...], jnp.concatenate([high, rest], axis=1), preferred_element_type=F32)
        send[it, group] = (whole[:, :128] + whole[:, 128:]).reshape(n, rows, 128)
        if narrow:
            low_send[group] = send[it, group].astype(BF16)
        for d in range(1, n):
            target = lax.rem(me + d, n)
            if narrow:
                push(
                    low_send.at[group, target], low_recv.at[group, d - 1], s_sem.at[it, group], r_sem.at[it, group],
                    {axis: target},
                )
                continue
            push(
                send.at[it, group, target], recv.at[it, group, d - 1], s_sem.at[it, group], r_sem.at[it, group],
                {axis: target},
            )

    def scatter_wait(it, group, matrix, rows, send, recv, me, n, axis, s_sem, r_sem, narrow=False):
        total = send[it, group, me]
        if narrow:
            drain_low(r_sem, it, group)
        else:
            drain(recv, r_sem, it, group)
        for d in range(1, n):
            total = total + (low_recv[group, d - 1].astype(F32) if narrow else recv[it, group, d - 1])
        return total

    lanes = slots * HALF

    def build(index_v, matrix):
        slot = lax.broadcasted_iota(jnp.int32, (8, slots), 1)
        place = jnp.where(slot < count_s[0], jnp.broadcast_to(index_v[...], (8, slots)), -1)
        lane = lax.broadcasted_iota(jnp.int32, (slots, lanes), 1)
        wider = (lane // HALF == lax.broadcasted_iota(jnp.int32, (slots, lanes), 0)).astype(F32).astype(BF16)
        place = jnp.dot(place.astype(F32).astype(BF16), wider, preferred_element_type=F32)
        sub = lax.broadcasted_iota(jnp.int32, (8, lanes), 0)
        own = lax.broadcasted_iota(jnp.int32, (8, lanes), 1) % HALF == sub % HALF
        place = jnp.where(own, place, -100000.0).astype(jnp.int32) - sub // HALF
        two = jnp.concatenate([place, place - 2], axis=0)

        def step(c, carry):
            matrix[pl.ds(pl.multiple_of(c * 16, 16), 16), :] = jnp.where(two == 4 * c, 1.0, 0.0).astype(BF16)
            return carry

        lax.fori_loop(0, matrix.shape[0] // 16, step, 0)

    y_args = (y_tiles, y_send, y_recv, y_full, me_j, n_col, "col", ys_sem, yr_sem)
    x_args = (x_tiles, x_send, x_recv, x_full, me_i, n_row, "row", xs_sem, xr_sem)
    g_args = (spread_g, x_tiles * HALF, g_send, g_recv, me_i, n_row, "row", gs_sem, gr_sem)
    h_args = (spread_h, y_tiles * HALF, h_send, h_recv, me_j, n_col, "col", hs_sem, hr_sem)

    loads[0].wait()
    for group in range(GROUPS):
        y_st[group] = to_rows(y_v, group, y_tiles)
    pl.semaphore_wait(barrier, n_row + n_col - 2)
    for group in range(GROUPS):
        gather_start(0, group, y_st[group], *y_args)
    for load in loads[1:]:
        load.wait()
    build(cols_v, spread_g)
    for group in range(GROUPS):
        x_st[group] = to_rows(x_v, group, x_tiles)
        cost_st[group] = to_rows(cost_v, group, x_tiles)
    upper_st[...] = spread_rows(upper_v, x_tiles)
    rhs_st[...] = spread_rows(rhs_v, y_tiles)
    kind_st[...] = spread_rows(kind_v, y_tiles)
    stores = (pltpu.make_async_copy(x_v, out_x_h, out_sem.at[0]), pltpu.make_async_copy(y_v, out_y_h, out_sem.at[1]))
    for it in range(ITERS):
        last = it == ITERS - 1
        for group in range(GROUPS):
            gather_wait(it, group, *y_args)
            products(it, group, y_full, rows_s, tiles_v)
            scatter_start(it, group, *g_args)
        if it == 0:
            for s in range(slots):
                turned[s] = tiles_v[s].T
            build(rows_v, spread_h)
        for group in range(GROUPS):
            grad = scatter_wait(it, group, *g_args)
            x = x_st[group]
            moved = x - PRIMAL_STEP * (cost_st[group] - grad)
            x_new = jnp.minimum(jnp.maximum(moved, 0.0), upper_st[...])
            gather_start(it, group, 2.0 * x_new - x, *x_args)
            x_st[group] = x_new
            if last:
                from_rows(x_v, group, x_new, x_tiles)
        if last:
            stores[0].start()
        for group in range(GROUPS):
            gather_wait(it, group, *x_args)
            products(it, group, x_full, cols_s, turned)
            scatter_start(it, group, *h_args, narrow=last)
        for group in range(GROUPS):
            image = scatter_wait(it, group, *h_args, narrow=last)
            y_new = y_st[group] + DUAL_STEP * (rhs_st[...] - image)
            y_new = jnp.where(kind_st[...] == 1, jnp.maximum(y_new, 0.0), y_new)
            if last:
                from_rows(y_v, group, y_new, y_tiles)
            else:
                y_st[group] = y_new
                gather_start(it + 1, group, y_new, *y_args)
    stores[1].start()
    for it in range(ITERS):
        for group in range(GROUPS):
            drain(y_recv, ys_sem, it, group)
            drain(g_recv, gs_sem, it, group)
            drain(x_recv, xs_sem, it, group)
            if it == ITERS - 1:
                drain_low(hs_sem, it, group)
            else:
                drain(h_recv, hs_sem, it, group)
    for store in stores:
        store.wait()


def body(primal, dual, cost, upper, rhs, row_kind, tiles, tile_rows, tile_cols, tile_count):
    n_row = lax.axis_size("row")
    n_col = lax.axis_size("col")
    x_width, y_width = primal.shape[1], dual.shape[1]
    slots = tiles.shape[0]
    x_rows, y_rows = x_width // 128 * HALF, y_width // 128 * HALF
    any_spec = pl.BlockSpec(memory_space=pl.ANY)
    dma = pltpu.SemaphoreType.DMA
    both = (ITERS, GROUPS)

    def exchange(n, rows):
        return [
            pltpu.VMEM(both + (rows, 128), BF16), pltpu.VMEM(both + (n - 1, rows, 128), BF16),
            pltpu.VMEM(both + (n * rows // HALF, 8, 128), F32),
        ]

    def partial(n, rows):
        return [pltpu.VMEM(both + (n, rows, 128), F32), pltpu.VMEM(both + (n - 1, rows, 128), F32)]

    scratch = [
        pltpu.VMEM((8, x_width), F32), pltpu.VMEM((8, y_width), F32), pltpu.VMEM((8, x_width), F32),
        pltpu.VMEM((1, x_width), F32), pltpu.VMEM((1, y_width), F32), pltpu.VMEM((1, y_width), jnp.int32),
        pltpu.VMEM(tiles.shape, BF16), pltpu.VMEM((1, slots), jnp.int32), pltpu.VMEM((1, slots), jnp.int32),
        pltpu.SMEM((1, slots), jnp.int32), pltpu.SMEM((1, slots), jnp.int32),
        pltpu.VMEM((GROUPS, x_rows, 128), F32), pltpu.VMEM((GROUPS, y_rows, 128), F32),
        pltpu.VMEM((GROUPS, x_rows, 128), F32), pltpu.VMEM((x_rows, 128), F32),
        pltpu.VMEM((y_rows, 128), F32), pltpu.VMEM((y_rows, 128), jnp.int32),
        pltpu.VMEM(tiles.shape, BF16),
        pltpu.VMEM((x_rows * n_row, slots * HALF), BF16), pltpu.VMEM((y_rows * n_col, slots * HALF), BF16),
        pltpu.VMEM((GROUPS, slots * HALF, 128), F32),
    ]
    scratch += exchange(n_col, y_rows) + exchange(n_row, x_rows) + partial(n_row, x_rows) + partial(n_col, y_rows)
    scratch += [pltpu.VMEM((GROUPS, n_col, y_rows, 128), BF16), pltpu.VMEM((GROUPS, n_col - 1, y_rows, 128), BF16)]
    scratch += [dma((11,)), dma((2,))] + [dma(both)] * 8
    operands = [
        pltpu.with_memory_space_constraint(operand, pltpu.HBM)
        for operand in (
            primal, dual, cost, upper.reshape(1, -1), rhs.reshape(1, -1), row_kind.reshape(1, -1), tiles,
            tile_rows.reshape(1, -1), tile_cols.reshape(1, -1),
        )
    ]
    return pl.pallas_call(
        functools.partial(kernel, n_row, n_col),
        out_shape=(jax.ShapeDtypeStruct(primal.shape, F32), jax.ShapeDtypeStruct(dual.shape, F32)),
        in_specs=[any_spec] * 9 + [pl.BlockSpec(memory_space=pltpu.SMEM)],
        out_specs=(any_spec, any_spec),
        scratch_shapes=scratch,
        compiler_params=pltpu.CompilerParams(
            collective_id=0, has_side_effects=True, vmem_limit_bytes=40 * 1024 * 1024,
        ),
        name="pdhg",
    )(
        *operands, tile_count,
    )


def solution(mesh):
    in_specs = (
        P(None, ("col", "row")),
        P(None, ("row", "col")),
        P(None, ("col", "row")),
        P(("col", "row")),
        P(("row", "col")),
        P(("row", "col")),
        P(("row", "col"), None, None),
        P(("row", "col")),
        P(("row", "col")),
        P(("row", "col")),
    )
    out_specs = (P(None, ("col", "row")), P(None, ("row", "col")))
    return jax.shard_map(body, mesh=mesh, in_specs=in_specs, out_specs=out_specs, check_vma=False)
```

```python
import functools

import jax
import jax.numpy as jnp
from jax import lax
from jax.experimental import pallas as pl
from jax.experimental.pallas import tpu as pltpu
from jax.sharding import PartitionSpec as P

ITERS = 2
GROUPS = 4
HALF = 2
PRIMAL_STEP = 0.4
DUAL_STEP = 0.4
BF16 = jnp.bfloat16
F32 = jnp.float32


def kernel(
    n_row, n_col,
    primal_h, dual_h, cost_h, upper_h, rhs_h, kind_h, tiles_h, rows_h, cols_h, count_s,
    out_x_h, out_y_h,
    x_v, y_v, cost_v, upper_v, rhs_v, kind_v, tiles_v, rows_v, cols_v, rows_s, cols_s,
    x_st, y_st, cost_st, upper_st, rhs_st, kind_st,
    turned, spread_g, spread_h, contrib,
    y_send, y_recv, y_full, x_send, x_recv, x_full,
    g_send, g_recv, h_send, h_recv, low_send, low_recv,
    in_sem, out_sem, ys_sem, yr_sem, gs_sem, gr_sem, xs_sem, xr_sem, hs_sem, hr_sem,
):
    me_i = lax.axis_index("row")
    me_j = lax.axis_index("col")
    slots = tiles_v.shape[0]
    x_tiles = x_v.shape[1] // 128
    y_tiles = y_v.shape[1] // 128

    barrier = pltpu.get_barrier_semaphore()
    for d in range(1, n_col):
        pl.semaphore_signal(barrier, inc=1, device_id={"col": lax.rem(me_j + d, n_col)}, device_id_type=pl.DeviceIdType.MESH)
    for d in range(1, n_row):
        pl.semaphore_signal(barrier, inc=1, device_id={"row": lax.rem(me_i + d, n_row)}, device_id_type=pl.DeviceIdType.MESH)

    loads = [
        pltpu.make_async_copy(src, dst, in_sem.at[k])
        for k, (src, dst) in enumerate((
            (dual_h, y_v), (cols_h, cols_v), (rows_h, rows_v), (tiles_h, tiles_v), (primal_h, x_v),
            (cost_h, cost_v), (upper_h, upper_v), (rhs_h, rhs_v), (kind_h, kind_v),
            (rows_h, rows_s), (cols_h, cols_s),
        ))
    ]
    for load in loads:
        load.start()

    def to_rows(ref, group, tiles):
        return jnp.concatenate(
            [ref[group * HALF:(group + 1) * HALF, t * 128:(t + 1) * 128] for t in range(tiles)], axis=0
        )

    def spread_rows(ref, tiles):
        return jnp.concatenate(
            [jnp.broadcast_to(ref[:, t * 128:(t + 1) * 128], (HALF, 128)) for t in range(tiles)], axis=0
        )

    def from_rows(ref, group, value, tiles):
        for t in range(tiles):
            ref[group * HALF:(group + 1) * HALF, t * 128:(t + 1) * 128] = value[t * HALF:(t + 1) * HALF]

    def push(src, dst, send_sem, recv_sem, device):
        pltpu.make_async_remote_copy(
            src_ref=src, dst_ref=dst, send_sem=send_sem, recv_sem=recv_sem,
            device_id=device, device_id_type=pl.DeviceIdType.MESH,
        ).start()

    def drain(recv, sem, it, group):
        whole = recv.at[it, group]
        pltpu.make_async_copy(whole, whole, sem.at[it, group]).wait()

    def drain_low(sem, it, group):
        whole = low_recv.at[group]
        pltpu.make_async_copy(whole, whole, sem.at[it, group]).wait()

    def fill(full, it, group, first, value, tiles):
        for t in range(tiles):
            part = value[t * HALF:(t + 1) * HALF]
            full[it, group, first + t] = jnp.concatenate([part, part], axis=0)

    def gather_start(it, group, value, tiles, send, recv, full, me, n, axis, s_sem, r_sem):
        low = value.astype(BF16)
        send[it, group] = low
        for d in range(1, n):
            push(
                send.at[it, group], recv.at[it, group, d - 1], s_sem.at[it, group], r_sem.at[it, group],
                {axis: lax.rem(me + d, n)},
            )
        fill(full, it, group, me * tiles, low.astype(F32), tiles)

    def gather_wait(it, group, tiles, send, recv, full, me, n, axis, s_sem, r_sem):
        drain(recv, r_sem, it, group)
        for d in range(1, n):
            source = lax.rem(me + n - d, n)
            fill(full, it, group, source * tiles, recv[it, group, d - 1].astype(F32), tiles)

    upper_half = lax.broadcasted_iota(jnp.int32, (2 * HALF, 128), 0) < HALF

    def products(it, group, full, index, blocks):
        for s in range(0, slots, 2):
            one = jnp.where(upper_half, full[it, group, index[0, s]], 0.0)
            two = jnp.where(upper_half, 0.0, full[it, group, index[0, s + 1]])
            left = jnp.concatenate([one, two], axis=1).astype(BF16)
            both = jnp.dot(left, blocks[s:s + 2].reshape(256, 128), preferred_element_type=F32)
            contrib[group, s * HALF:(s + 2) * HALF, :] = both

    def scatter_start(it, group, matrix, rows, send, recv, me, n, axis, s_sem, r_sem, narrow=False):
        terms = contrib[group]
        high = terms.astype(BF16)
        rest = (terms - high.astype(F32)).astype(BF16)
        whole = jnp.dot(matrix[...], jnp.concatenate([high, rest], axis=1), preferred_element_type=F32)
        send[it, group] = (whole[:, :128] + whole[:, 128:]).reshape(n, rows, 128)
        if narrow:
            low_send[group] = send[it, group].astype(BF16)
        for d in range(1, n):
            target = lax.rem(me + d, n)
            if narrow:
                push(
                    low_send.at[group, target], low_recv.at[group, d - 1], s_sem.at[it, group], r_sem.at[it, group],
                    {axis: target},
                )
                continue
            push(
                send.at[it, group, target], recv.at[it, group, d - 1], s_sem.at[it, group], r_sem.at[it, group],
                {axis: target},
            )

    def scatter_wait(it, group, matrix, rows, send, recv, me, n, axis, s_sem, r_sem, narrow=False):
        total = send[it, group, me]
        if narrow:
            drain_low(r_sem, it, group)
        else:
            drain(recv, r_sem, it, group)
        for d in range(1, n):
            total = total + (low_recv[group, d - 1].astype(F32) if narrow else recv[it, group, d - 1])
        return total

    lanes = slots * HALF

    def build(index_v, matrix):
        slot = lax.broadcasted_iota(jnp.int32, (8, slots), 1)
        place = jnp.where(slot < count_s[0], jnp.broadcast_to(index_v[...], (8, slots)), -1)
        lane = lax.broadcasted_iota(jnp.int32, (slots, lanes), 1)
        wider = (lane // HALF == lax.broadcasted_iota(jnp.int32, (slots, lanes), 0)).astype(F32).astype(BF16)
        place = jnp.dot(place.astype(F32).astype(BF16), wider, preferred_element_type=F32)
        sub = lax.broadcasted_iota(jnp.int32, (8, lanes), 0)
        own = lax.broadcasted_iota(jnp.int32, (8, lanes), 1) % HALF == sub % HALF
        place = jnp.where(own, place, -100000.0).astype(jnp.int32) - sub // HALF
        two = jnp.concatenate([place, place - 8 // HALF], axis=0)

        def step(c, carry):
            matrix[pl.ds(pl.multiple_of(c * 16, 16), 16), :] = jnp.where(two == 16 // HALF * c, 1.0, 0.0).astype(BF16)
            return carry

        lax.fori_loop(0, matrix.shape[0] // 16, step, 0)

    y_args = (y_tiles, y_send, y_recv, y_full, me_j, n_col, "col", ys_sem, yr_sem)
    x_args = (x_tiles, x_send, x_recv, x_full, me_i, n_row, "row", xs_sem, xr_sem)
    g_args = (spread_g, x_tiles * HALF, g_send, g_recv, me_i, n_row, "row", gs_sem, gr_sem)
    h_args = (spread_h, y_tiles * HALF, h_send, h_recv, me_j, n_col, "col", hs_sem, hr_sem)

    loads[0].wait()
    for group in range(GROUPS):
        y_st[group] = to_rows(y_v, group, y_tiles)
    pl.semaphore_wait(barrier, n_row + n_col - 2)
    for group in range(GROUPS):
        gather_start(0, group, y_st[group], *y_args)
    for load in loads[1:]:
        load.wait()
    build(cols_v, spread_g)
    for group in range(GROUPS):
        x_st[group] = to_rows(x_v, group, x_tiles)
        cost_st[group] = to_rows(cost_v, group, x_tiles)
    upper_st[...] = spread_rows(upper_v, x_tiles)
    rhs_st[...] = spread_rows(rhs_v, y_tiles)
    kind_st[...] = spread_rows(kind_v, y_tiles)
    stores = (pltpu.make_async_copy(x_v, out_x_h, out_sem.at[0]), pltpu.make_async_copy(y_v, out_y_h, out_sem.at[1]))
    for it in range(ITERS):
        last = it == ITERS - 1
        for group in range(GROUPS):
            gather_wait(it, group, *y_args)
            products(it, group, y_full, rows_s, tiles_v)
            scatter_start(it, group, *g_args)
        if it == 0:
            for s in range(slots):
                turned[s] = tiles_v[s].T
            build(rows_v, spread_h)
        for group in range(GROUPS):
            grad = scatter_wait(it, group, *g_args)
            x = x_st[group]
            moved = x - PRIMAL_STEP * (cost_st[group] - grad)
            x_new = jnp.minimum(jnp.maximum(moved, 0.0), upper_st[...])
            gather_start(it, group, 2.0 * x_new - x, *x_args)
            x_st[group] = x_new
            if last:
                from_rows(x_v, group, x_new, x_tiles)
        if last:
            stores[0].start()
        for group in range(GROUPS):
            gather_wait(it, group, *x_args)
            products(it, group, x_full, cols_s, turned)
            scatter_start(it, group, *h_args, narrow=last)
        for group in range(GROUPS):
            image = scatter_wait(it, group, *h_args, narrow=last)
            y_new = y_st[group] + DUAL_STEP * (rhs_st[...] - image)
            y_new = jnp.where(kind_st[...] == 1, jnp.maximum(y_new, 0.0), y_new)
            if last:
                from_rows(y_v, group, y_new, y_tiles)
            else:
                y_st[group] = y_new
                gather_start(it + 1, group, y_new, *y_args)
    stores[1].start()
    for it in range(ITERS):
        for group in range(GROUPS):
            drain(y_recv, ys_sem, it, group)
            drain(g_recv, gs_sem, it, group)
            drain(x_recv, xs_sem, it, group)
            if it == ITERS - 1:
                drain_low(hs_sem, it, group)
            else:
                drain(h_recv, hs_sem, it, group)
    for store in stores:
        store.wait()


def body(primal, dual, cost, upper, rhs, row_kind, tiles, tile_rows, tile_cols, tile_count):
    n_row = lax.axis_size("row")
    n_col = lax.axis_size("col")
    x_width, y_width = primal.shape[1], dual.shape[1]
    slots = tiles.shape[0]
    x_rows, y_rows = x_width // 128 * HALF, y_width // 128 * HALF
    any_spec = pl.BlockSpec(memory_space=pl.ANY)
    dma = pltpu.SemaphoreType.DMA
    both = (ITERS, GROUPS)

    def exchange(n, rows):
        return [
            pltpu.VMEM(both + (rows, 128), BF16), pltpu.VMEM(both + (n - 1, rows, 128), BF16),
            pltpu.VMEM(both + (n * rows // HALF, 2 * HALF, 128), F32),
        ]

    def partial(n, rows):
        return [pltpu.VMEM(both + (n, rows, 128), F32), pltpu.VMEM(both + (n - 1, rows, 128), F32)]

    scratch = [
        pltpu.VMEM((8, x_width), F32), pltpu.VMEM((8, y_width), F32), pltpu.VMEM((8, x_width), F32),
        pltpu.VMEM((1, x_width), F32), pltpu.VMEM((1, y_width), F32), pltpu.VMEM((1, y_width), jnp.int32),
        pltpu.VMEM(tiles.shape, BF16), pltpu.VMEM((1, slots), jnp.int32), pltpu.VMEM((1, slots), jnp.int32),
        pltpu.SMEM((1, slots), jnp.int32), pltpu.SMEM((1, slots), jnp.int32),
        pltpu.VMEM((GROUPS, x_rows, 128), F32), pltpu.VMEM((GROUPS, y_rows, 128), F32),
        pltpu.VMEM((GROUPS, x_rows, 128), F32), pltpu.VMEM((x_rows, 128), F32),
        pltpu.VMEM((y_rows, 128), F32), pltpu.VMEM((y_rows, 128), jnp.int32),
        pltpu.VMEM(tiles.shape, BF16),
        pltpu.VMEM((x_rows * n_row, slots * HALF), BF16), pltpu.VMEM((y_rows * n_col, slots * HALF), BF16),
        pltpu.VMEM((GROUPS, slots * HALF, 128), F32),
    ]
    scratch += exchange(n_col, y_rows) + exchange(n_row, x_rows) + partial(n_row, x_rows) + partial(n_col, y_rows)
    scratch += [pltpu.VMEM((GROUPS, n_col, y_rows, 128), BF16), pltpu.VMEM((GROUPS, n_col - 1, y_rows, 128), BF16)]
    scratch += [dma((11,)), dma((2,))] + [dma(both)] * 8
    operands = [
        pltpu.with_memory_space_constraint(operand, pltpu.HBM)
        for operand in (
            primal, dual, cost, upper.reshape(1, -1), rhs.reshape(1, -1), row_kind.reshape(1, -1), tiles,
            tile_rows.reshape(1, -1), tile_cols.reshape(1, -1),
        )
    ]
    return pl.pallas_call(
        functools.partial(kernel, n_row, n_col),
        out_shape=(jax.ShapeDtypeStruct(primal.shape, F32), jax.ShapeDtypeStruct(dual.shape, F32)),
        in_specs=[any_spec] * 9 + [pl.BlockSpec(memory_space=pltpu.SMEM)],
        out_specs=(any_spec, any_spec),
        scratch_shapes=scratch,
        compiler_params=pltpu.CompilerParams(
            collective_id=0, has_side_effects=True, vmem_limit_bytes=40 * 1024 * 1024,
        ),
        name="pdhg",
    )(
        *operands, tile_count,
    )


def solution(mesh):
    in_specs = (
        P(None, ("col", "row")),
        P(None, ("row", "col")),
        P(None, ("col", "row")),
        P(("col", "row")),
        P(("row", "col")),
        P(("row", "col")),
        P(("row", "col"), None, None),
        P(("row", "col")),
        P(("row", "col")),
        P(("row", "col")),
    )
    out_specs = (P(None, ("col", "row")), P(None, ("row", "col")))
    return jax.shard_map(body, mesh=mesh, in_specs=in_specs, out_specs=out_specs, check_vma=False)
```

```python
import functools

import jax
import jax.numpy as jnp
from jax import lax
from jax.experimental import pallas as pl
from jax.experimental.pallas import tpu as pltpu
from jax.sharding import PartitionSpec as P

ITERS = 2
GROUPS = 2
HALF = 4
PRIMAL_STEP = 0.4
DUAL_STEP = 0.4
BF16 = jnp.bfloat16
F32 = jnp.float32


def kernel(
    n_row, n_col,
    primal_h, dual_h, cost_h, upper_h, rhs_h, kind_h, tiles_h, rows_h, cols_h, count_s,
    out_x_h, out_y_h,
    x_v, y_v, cost_v, upper_v, rhs_v, kind_v, tiles_v, rows_v, cols_v, rows_s, cols_s,
    x_st, y_st, cost_st, upper_st, rhs_st, kind_st,
    turned, spread_g, spread_h, contrib,
    y_send, y_recv, y_full, x_send, x_recv, x_full,
    g_send, g_recv, h_send, h_recv, low_send, low_recv,
    in_sem, out_sem, ys_sem, yr_sem, gs_sem, gr_sem, xs_sem, xr_sem, hs_sem, hr_sem,
):
    me_i = lax.axis_index("row")
    me_j = lax.axis_index("col")
    slots = tiles_v.shape[0]
    x_tiles = x_v.shape[1] // 128
    y_tiles = y_v.shape[1] // 128

    barrier = pltpu.get_barrier_semaphore()
    for d in range(1, n_col):
        pl.semaphore_signal(barrier, inc=1, device_id={"col": lax.rem(me_j + d, n_col)}, device_id_type=pl.DeviceIdType.MESH)
    for d in range(1, n_row):
        pl.semaphore_signal(barrier, inc=1, device_id={"row": lax.rem(me_i + d, n_row)}, device_id_type=pl.DeviceIdType.MESH)

    loads = [
        pltpu.make_async_copy(src, dst, in_sem.at[k])
        for k, (src, dst) in enumerate((
            (dual_h, y_v), (cols_h, cols_v), (rows_h, rows_v), (tiles_h, tiles_v), (primal_h, x_v),
            (cost_h, cost_v), (upper_h, upper_v), (rhs_h, rhs_v), (kind_h, kind_v),
            (rows_h, rows_s), (cols_h, cols_s),
        ))
    ]
    for load in loads:
        load.start()

    def to_rows(ref, group, tiles):
        return jnp.concatenate(
            [ref[group * HALF:(group + 1) * HALF, t * 128:(t + 1) * 128] for t in range(tiles)], axis=0
        )

    def spread_rows(ref, tiles):
        return jnp.concatenate(
            [jnp.broadcast_to(ref[:, t * 128:(t + 1) * 128], (HALF, 128)) for t in range(tiles)], axis=0
        )

    def from_rows(ref, group, value, tiles):
        for t in range(tiles):
            ref[group * HALF:(group + 1) * HALF, t * 128:(t + 1) * 128] = value[t * HALF:(t + 1) * HALF]

    def push(src, dst, send_sem, recv_sem, device):
        pltpu.make_async_remote_copy(
            src_ref=src, dst_ref=dst, send_sem=send_sem, recv_sem=recv_sem,
            device_id=device, device_id_type=pl.DeviceIdType.MESH,
        ).start()

    def drain(recv, sem, it, group):
        whole = recv.at[it, group]
        pltpu.make_async_copy(whole, whole, sem.at[it, group]).wait()

    def drain_low(sem, it, group):
        whole = low_recv.at[group]
        pltpu.make_async_copy(whole, whole, sem.at[it, group]).wait()

    def fill(full, it, group, first, value, tiles):
        for t in range(tiles):
            part = value[t * HALF:(t + 1) * HALF]
            full[it, group, first + t] = jnp.concatenate([part, part], axis=0)

    def gather_start(it, group, value, tiles, send, recv, full, me, n, axis, s_sem, r_sem):
        low = value.astype(BF16)
        send[it, group] = low
        for d in range(1, n):
            push(
                send.at[it, group], recv.at[it, group, d - 1], s_sem.at[it, group], r_sem.at[it, group],
                {axis: lax.rem(me + d, n)},
            )
        fill(full, it, group, me * tiles, low.astype(F32), tiles)

    def gather_wait(it, group, tiles, send, recv, full, me, n, axis, s_sem, r_sem):
        drain(recv, r_sem, it, group)
        for d in range(1, n):
            source = lax.rem(me + n - d, n)
            fill(full, it, group, source * tiles, recv[it, group, d - 1].astype(F32), tiles)

    upper_half = lax.broadcasted_iota(jnp.int32, (2 * HALF, 128), 0) < HALF

    def products(it, group, full, index, blocks):
        zero = jnp.zeros((2 * HALF, 128), F32)
        for s in range(0, slots, 4):
            one = jnp.where(upper_half, full[it, group, index[0, s]], full[it, group, index[0, s + 1]])
            two = jnp.where(upper_half, full[it, group, index[0, s + 2]], full[it, group, index[0, s + 3]])
            left = jnp.concatenate(
                [jnp.concatenate([one, zero], axis=0), jnp.concatenate([zero, two], axis=0)], axis=1
            ).astype(BF16)
            right = jnp.concatenate(
                [
                    jnp.concatenate([blocks[s], blocks[s + 2]], axis=0),
                    jnp.concatenate([blocks[s + 1], blocks[s + 3]], axis=0),
                ],
                axis=1,
            )
            four = jnp.dot(left, right, preferred_element_type=F32)
            for k in range(2):
                half = four[2 * HALF * k:2 * HALF * (k + 1)]
                contrib[group, (s + 2 * k) * HALF:(s + 2 * k + 2) * HALF, :] = jnp.where(
                    upper_half, half[:, :128], half[:, 128:]
                )

    def scatter_start(it, group, matrix, rows, send, recv, me, n, axis, s_sem, r_sem, narrow=False):
        terms = contrib[group]
        high = terms.astype(BF16)
        rest = (terms - high.astype(F32)).astype(BF16)
        whole = jnp.dot(matrix[...], jnp.concatenate([high, rest], axis=1), preferred_element_type=F32)
        send[it, group] = (whole[:, :128] + whole[:, 128:]).reshape(n, rows, 128)
        if narrow:
            low_send[group] = send[it, group].astype(BF16)
        for d in range(1, n):
            target = lax.rem(me + d, n)
            if narrow:
                push(
                    low_send.at[group, target], low_recv.at[group, d - 1], s_sem.at[it, group], r_sem.at[it, group],
                    {axis: target},
                )
                continue
            push(
                send.at[it, group, target], recv.at[it, group, d - 1], s_sem.at[it, group], r_sem.at[it, group],
                {axis: target},
            )

    def scatter_wait(it, group, matrix, rows, send, recv, me, n, axis, s_sem, r_sem, narrow=False):
        total = send[it, group, me]
        if narrow:
            drain_low(r_sem, it, group)
        else:
            drain(recv, r_sem, it, group)
        for d in range(1, n):
            total = total + (low_recv[group, d - 1].astype(F32) if narrow else recv[it, group, d - 1])
        return total

    lanes = slots * HALF

    def build(index_v, matrix):
        slot = lax.broadcasted_iota(jnp.int32, (8, slots), 1)
        place = jnp.where(slot < count_s[0], jnp.broadcast_to(index_v[...], (8, slots)), -1)
        lane = lax.broadcasted_iota(jnp.int32, (slots, lanes), 1)
        wider = (lane // HALF == lax.broadcasted_iota(jnp.int32, (slots, lanes), 0)).astype(F32).astype(BF16)
        place = jnp.dot(place.astype(F32).astype(BF16), wider, preferred_element_type=F32)
        sub = lax.broadcasted_iota(jnp.int32, (8, lanes), 0)
        own = lax.broadcasted_iota(jnp.int32, (8, lanes), 1) % HALF == sub % HALF
        place = jnp.where(own, place, -100000.0).astype(jnp.int32) - sub // HALF
        two = jnp.concatenate([place, place - 8 // HALF], axis=0)

        def step(c, carry):
            matrix[pl.ds(pl.multiple_of(c * 16, 16), 16), :] = jnp.where(two == 16 // HALF * c, 1.0, 0.0).astype(BF16)
            return carry

        lax.fori_loop(0, matrix.shape[0] // 16, step, 0)

    y_args = (y_tiles, y_send, y_recv, y_full, me_j, n_col, "col", ys_sem, yr_sem)
    x_args = (x_tiles, x_send, x_recv, x_full, me_i, n_row, "row", xs_sem, xr_sem)
    g_args = (spread_g, x_tiles * HALF, g_send, g_recv, me_i, n_row, "row", gs_sem, gr_sem)
    h_args = (spread_h, y_tiles * HALF, h_send, h_recv, me_j, n_col, "col", hs_sem, hr_sem)

    loads[0].wait()
    for group in range(GROUPS):
        y_st[group] = to_rows(y_v, group, y_tiles)
    pl.semaphore_wait(barrier, n_row + n_col - 2)
    for group in range(GROUPS):
        gather_start(0, group, y_st[group], *y_args)
    for load in loads[1:]:
        load.wait()
    build(cols_v, spread_g)
    for group in range(GROUPS):
        x_st[group] = to_rows(x_v, group, x_tiles)
        cost_st[group] = to_rows(cost_v, group, x_tiles)
    upper_st[...] = spread_rows(upper_v, x_tiles)
    rhs_st[...] = spread_rows(rhs_v, y_tiles)
    kind_st[...] = spread_rows(kind_v, y_tiles)
    stores = (pltpu.make_async_copy(x_v, out_x_h, out_sem.at[0]), pltpu.make_async_copy(y_v, out_y_h, out_sem.at[1]))
    for it in range(ITERS):
        last = it == ITERS - 1
        for group in range(GROUPS):
            gather_wait(it, group, *y_args)
            products(it, group, y_full, rows_s, tiles_v)
            scatter_start(it, group, *g_args)
        if it == 0:
            for s in range(slots):
                turned[s] = tiles_v[s].T
            build(rows_v, spread_h)
        for group in range(GROUPS):
            grad = scatter_wait(it, group, *g_args)
            x = x_st[group]
            moved = x - PRIMAL_STEP * (cost_st[group] - grad)
            x_new = jnp.minimum(jnp.maximum(moved, 0.0), upper_st[...])
            gather_start(it, group, 2.0 * x_new - x, *x_args)
            x_st[group] = x_new
            if last:
                from_rows(x_v, group, x_new, x_tiles)
        if last:
            stores[0].start()
        for group in range(GROUPS):
            gather_wait(it, group, *x_args)
            products(it, group, x_full, cols_s, turned)
            scatter_start(it, group, *h_args, narrow=last)
        for group in range(GROUPS):
            image = scatter_wait(it, group, *h_args, narrow=last)
            y_new = y_st[group] + DUAL_STEP * (rhs_st[...] - image)
            y_new = jnp.where(kind_st[...] == 1, jnp.maximum(y_new, 0.0), y_new)
            if last:
                from_rows(y_v, group, y_new, y_tiles)
            else:
                y_st[group] = y_new
                gather_start(it + 1, group, y_new, *y_args)
    stores[1].start()
    for it in range(ITERS):
        for group in range(GROUPS):
            drain(y_recv, ys_sem, it, group)
            drain(g_recv, gs_sem, it, group)
            drain(x_recv, xs_sem, it, group)
            if it == ITERS - 1:
                drain_low(hs_sem, it, group)
            else:
                drain(h_recv, hs_sem, it, group)
    for store in stores:
        store.wait()


def body(primal, dual, cost, upper, rhs, row_kind, tiles, tile_rows, tile_cols, tile_count):
    n_row = lax.axis_size("row")
    n_col = lax.axis_size("col")
    x_width, y_width = primal.shape[1], dual.shape[1]
    slots = tiles.shape[0]
    x_rows, y_rows = x_width // 128 * HALF, y_width // 128 * HALF
    any_spec = pl.BlockSpec(memory_space=pl.ANY)
    dma = pltpu.SemaphoreType.DMA
    both = (ITERS, GROUPS)

    def exchange(n, rows):
        return [
            pltpu.VMEM(both + (rows, 128), BF16), pltpu.VMEM(both + (n - 1, rows, 128), BF16),
            pltpu.VMEM(both + (n * rows // HALF, 2 * HALF, 128), F32),
        ]

    def partial(n, rows):
        return [pltpu.VMEM(both + (n, rows, 128), F32), pltpu.VMEM(both + (n - 1, rows, 128), F32)]

    scratch = [
        pltpu.VMEM((8, x_width), F32), pltpu.VMEM((8, y_width), F32), pltpu.VMEM((8, x_width), F32),
        pltpu.VMEM((1, x_width), F32), pltpu.VMEM((1, y_width), F32), pltpu.VMEM((1, y_width), jnp.int32),
        pltpu.VMEM(tiles.shape, BF16), pltpu.VMEM((1, slots), jnp.int32), pltpu.VMEM((1, slots), jnp.int32),
        pltpu.SMEM((1, slots), jnp.int32), pltpu.SMEM((1, slots), jnp.int32),
        pltpu.VMEM((GROUPS, x_rows, 128), F32), pltpu.VMEM((GROUPS, y_rows, 128), F32),
        pltpu.VMEM((GROUPS, x_rows, 128), F32), pltpu.VMEM((x_rows, 128), F32),
        pltpu.VMEM((y_rows, 128), F32), pltpu.VMEM((y_rows, 128), jnp.int32),
        pltpu.VMEM(tiles.shape, BF16),
        pltpu.VMEM((x_rows * n_row, slots * HALF), BF16), pltpu.VMEM((y_rows * n_col, slots * HALF), BF16),
        pltpu.VMEM((GROUPS, slots * HALF, 128), F32),
    ]
    scratch += exchange(n_col, y_rows) + exchange(n_row, x_rows) + partial(n_row, x_rows) + partial(n_col, y_rows)
    scratch += [pltpu.VMEM((GROUPS, n_col, y_rows, 128), BF16), pltpu.VMEM((GROUPS, n_col - 1, y_rows, 128), BF16)]
    scratch += [dma((11,)), dma((2,))] + [dma(both)] * 8
    operands = [
        pltpu.with_memory_space_constraint(operand, pltpu.HBM)
        for operand in (
            primal, dual, cost, upper.reshape(1, -1), rhs.reshape(1, -1), row_kind.reshape(1, -1), tiles,
            tile_rows.reshape(1, -1), tile_cols.reshape(1, -1),
        )
    ]
    return pl.pallas_call(
        functools.partial(kernel, n_row, n_col),
        out_shape=(jax.ShapeDtypeStruct(primal.shape, F32), jax.ShapeDtypeStruct(dual.shape, F32)),
        in_specs=[any_spec] * 9 + [pl.BlockSpec(memory_space=pltpu.SMEM)],
        out_specs=(any_spec, any_spec),
        scratch_shapes=scratch,
        compiler_params=pltpu.CompilerParams(
            collective_id=0, has_side_effects=True, vmem_limit_bytes=40 * 1024 * 1024,
        ),
        name="pdhg",
    )(
        *operands, tile_count,
    )


def solution(mesh):
    in_specs = (
        P(None, ("col", "row")),
        P(None, ("row", "col")),
        P(None, ("col", "row")),
        P(("col", "row")),
        P(("row", "col")),
        P(("row", "col")),
        P(("row", "col"), None, None),
        P(("row", "col")),
        P(("row", "col")),
        P(("row", "col")),
    )
    out_specs = (P(None, ("col", "row")), P(None, ("row", "col")))
    return jax.shard_map(body, mesh=mesh, in_specs=in_specs, out_specs=out_specs, check_vma=False)
```

```python
import functools

import jax
import jax.numpy as jnp
from jax import lax
from jax.experimental import pallas as pl
from jax.experimental.pallas import tpu as pltpu
from jax.sharding import PartitionSpec as P

ITERS = 2
GROUPS = 4
HALF = 2
PRIMAL_STEP = 0.4
DUAL_STEP = 0.4
BF16 = jnp.bfloat16
F32 = jnp.float32


def kernel(
    n_row, n_col,
    primal_h, dual_h, cost_h, upper_h, rhs_h, kind_h, tiles_h, rows_h, cols_h, count_s,
    out_x_h, out_y_h,
    x_v, y_v, cost_v, upper_v, rhs_v, kind_v, tiles_v, rows_v, cols_v, rows_s, cols_s,
    x_st, y_st, cost_st, upper_st, rhs_st, kind_st,
    turned, spread_g, spread_h, contrib,
    y_send, y_recv, y_full, x_send, x_recv, x_full,
    g_send, g_recv, h_send, h_recv, low_send, low_recv,
    in_sem, out_sem, ys_sem, yr_sem, gs_sem, gr_sem, xs_sem, xr_sem, hs_sem, hr_sem,
):
    me_i = lax.axis_index("row")
    me_j = lax.axis_index("col")
    slots = tiles_v.shape[0]
    x_tiles = x_v.shape[1] // 128
    y_tiles = y_v.shape[1] // 128

    barrier = pltpu.get_barrier_semaphore()
    for d in range(1, n_col):
        pl.semaphore_signal(barrier, inc=1, device_id={"col": lax.rem(me_j + d, n_col)}, device_id_type=pl.DeviceIdType.MESH)
    for d in range(1, n_row):
        pl.semaphore_signal(barrier, inc=1, device_id={"row": lax.rem(me_i + d, n_row)}, device_id_type=pl.DeviceIdType.MESH)

    loads = [
        pltpu.make_async_copy(src, dst, in_sem.at[k])
        for k, (src, dst) in enumerate((
            (dual_h, y_v), (cols_h, cols_v), (rows_h, rows_v), (tiles_h, tiles_v), (primal_h, x_v),
            (cost_h, cost_v), (upper_h, upper_v), (rhs_h, rhs_v), (kind_h, kind_v),
            (rows_h, rows_s), (cols_h, cols_s),
        ))
    ]
    for load in loads:
        load.start()

    def to_rows(ref, group, tiles):
        return jnp.concatenate(
            [ref[group * HALF:(group + 1) * HALF, t * 128:(t + 1) * 128] for t in range(tiles)], axis=0
        )

    def spread_rows(ref, tiles):
        return jnp.concatenate(
            [jnp.broadcast_to(ref[:, t * 128:(t + 1) * 128], (HALF, 128)) for t in range(tiles)], axis=0
        )

    def from_rows(ref, group, value, tiles):
        for t in range(tiles):
            ref[group * HALF:(group + 1) * HALF, t * 128:(t + 1) * 128] = value[t * HALF:(t + 1) * HALF]

    def push(src, dst, send_sem, recv_sem, device):
        pltpu.make_async_remote_copy(
            src_ref=src, dst_ref=dst, send_sem=send_sem, recv_sem=recv_sem,
            device_id=device, device_id_type=pl.DeviceIdType.MESH,
        ).start()

    def drain(recv, sem, it, group):
        whole = recv.at[it, group]
        pltpu.make_async_copy(whole, whole, sem.at[it, group]).wait()

    def drain_low(sem, it, group):
        whole = low_recv.at[group]
        pltpu.make_async_copy(whole, whole, sem.at[it, group]).wait()

    def fill(full, it, group, first, value, tiles):
        for t in range(tiles):
            part = value[t * HALF:(t + 1) * HALF]
            full[it, group, first + t] = jnp.concatenate([part, part], axis=0)

    def gather_start(it, group, value, tiles, send, recv, full, me, n, axis, s_sem, r_sem):
        low = value.astype(BF16)
        send[it, group] = low
        for d in range(1, n):
            push(
                send.at[it, group], recv.at[it, group, d - 1], s_sem.at[it, group], r_sem.at[it, group],
                {axis: lax.rem(me + d, n)},
            )
        fill(full, it, group, me * tiles, low.astype(F32), tiles)

    def gather_wait(it, group, tiles, send, recv, full, me, n, axis, s_sem, r_sem):
        drain(recv, r_sem, it, group)
        for d in range(1, n):
            source = lax.rem(me + n - d, n)
            fill(full, it, group, source * tiles, recv[it, group, d - 1].astype(F32), tiles)

    upper_half = lax.broadcasted_iota(jnp.int32, (2 * HALF, 128), 0) < HALF

    def products(it, group, full, index, blocks):
        zero = jnp.zeros((2 * HALF, 128), F32)
        for s in range(0, slots, 4):
            one = jnp.where(upper_half, full[it, group, index[0, s]], full[it, group, index[0, s + 1]])
            two = jnp.where(upper_half, full[it, group, index[0, s + 2]], full[it, group, index[0, s + 3]])
            left = jnp.concatenate(
                [jnp.concatenate([one, zero], axis=0), jnp.concatenate([zero, two], axis=0)], axis=1
            ).astype(BF16)
            right = jnp.concatenate(
                [
                    jnp.concatenate([blocks[s], blocks[s + 2]], axis=0),
                    jnp.concatenate([blocks[s + 1], blocks[s + 3]], axis=0),
                ],
                axis=1,
            )
            four = jnp.dot(left, right, preferred_element_type=F32)
            for k in range(2):
                half = four[2 * HALF * k:2 * HALF * (k + 1)]
                contrib[group, (s + 2 * k) * HALF:(s + 2 * k + 2) * HALF, :] = jnp.where(
                    upper_half, half[:, :128], half[:, 128:]
                )

    def scatter_start(it, group, matrix, rows, send, recv, me, n, axis, s_sem, r_sem, narrow=False):
        terms = contrib[group]
        high = terms.astype(BF16)
        rest = (terms - high.astype(F32)).astype(BF16)
        whole = jnp.dot(matrix[...], jnp.concatenate([high, rest], axis=1), preferred_element_type=F32)
        send[it, group] = (whole[:, :128] + whole[:, 128:]).reshape(n, rows, 128)
        if narrow:
            low_send[group] = send[it, group].astype(BF16)
        for d in range(1, n):
            target = lax.rem(me + d, n)
            if narrow:
                push(
                    low_send.at[group, target], low_recv.at[group, d - 1], s_sem.at[it, group], r_sem.at[it, group],
                    {axis: target},
                )
                continue
            push(
                send.at[it, group, target], recv.at[it, group, d - 1], s_sem.at[it, group], r_sem.at[it, group],
                {axis: target},
            )

    def scatter_wait(it, group, matrix, rows, send, recv, me, n, axis, s_sem, r_sem, narrow=False):
        total = send[it, group, me]
        if narrow:
            drain_low(r_sem, it, group)
        else:
            drain(recv, r_sem, it, group)
        for d in range(1, n):
            total = total + (low_recv[group, d - 1].astype(F32) if narrow else recv[it, group, d - 1])
        return total

    lanes = slots * HALF

    def build(index_v, matrix):
        slot = lax.broadcasted_iota(jnp.int32, (8, slots), 1)
        place = jnp.where(slot < count_s[0], jnp.broadcast_to(index_v[...], (8, slots)), -1)
        lane = lax.broadcasted_iota(jnp.int32, (slots, lanes), 1)
        wider = (lane // HALF == lax.broadcasted_iota(jnp.int32, (slots, lanes), 0)).astype(F32).astype(BF16)
        place = jnp.dot(place.astype(F32).astype(BF16), wider, preferred_element_type=F32)
        sub = lax.broadcasted_iota(jnp.int32, (8, lanes), 0)
        own = lax.broadcasted_iota(jnp.int32, (8, lanes), 1) % HALF == sub % HALF
        place = jnp.where(own, place, -100000.0).astype(jnp.int32) - sub // HALF
        two = jnp.concatenate([place, place - 8 // HALF], axis=0)

        def step(c, carry):
            matrix[pl.ds(pl.multiple_of(c * 16, 16), 16), :] = jnp.where(two == 16 // HALF * c, 1.0, 0.0).astype(BF16)
            return carry

        lax.fori_loop(0, matrix.shape[0] // 16, step, 0)

    y_args = (y_tiles, y_send, y_recv, y_full, me_j, n_col, "col", ys_sem, yr_sem)
    x_args = (x_tiles, x_send, x_recv, x_full, me_i, n_row, "row", xs_sem, xr_sem)
    g_args = (spread_g, x_tiles * HALF, g_send, g_recv, me_i, n_row, "row", gs_sem, gr_sem)
    h_args = (spread_h, y_tiles * HALF, h_send, h_recv, me_j, n_col, "col", hs_sem, hr_sem)

    loads[0].wait()
    for group in range(GROUPS):
        y_st[group] = to_rows(y_v, group, y_tiles)
    pl.semaphore_wait(barrier, n_row + n_col - 2)
    for group in range(GROUPS):
        gather_start(0, group, y_st[group], *y_args)
    for load in loads[1:]:
        load.wait()
    build(cols_v, spread_g)
    for group in range(GROUPS):
        x_st[group] = to_rows(x_v, group, x_tiles)
        cost_st[group] = to_rows(cost_v, group, x_tiles)
    upper_st[...] = spread_rows(upper_v, x_tiles)
    rhs_st[...] = spread_rows(rhs_v, y_tiles)
    kind_st[...] = spread_rows(kind_v, y_tiles)
    stores = (pltpu.make_async_copy(x_v, out_x_h, out_sem.at[0]), pltpu.make_async_copy(y_v, out_y_h, out_sem.at[1]))
    for it in range(ITERS):
        last = it == ITERS - 1
        for group in range(GROUPS):
            gather_wait(it, group, *y_args)
            products(it, group, y_full, rows_s, tiles_v)
            scatter_start(it, group, *g_args)
        if it == 0:
            for s in range(slots):
                turned[s] = tiles_v[s].T
            build(rows_v, spread_h)
        for group in range(GROUPS):
            grad = scatter_wait(it, group, *g_args)
            x = x_st[group]
            moved = x - PRIMAL_STEP * (cost_st[group] - grad)
            x_new = jnp.minimum(jnp.maximum(moved, 0.0), upper_st[...])
            gather_start(it, group, 2.0 * x_new - x, *x_args)
            x_st[group] = x_new
            if last:
                from_rows(x_v, group, x_new, x_tiles)
        if last:
            stores[0].start()
        for group in range(GROUPS):
            gather_wait(it, group, *x_args)
            products(it, group, x_full, cols_s, turned)
            scatter_start(it, group, *h_args, narrow=last)
        for group in range(GROUPS):
            image = scatter_wait(it, group, *h_args, narrow=last)
            y_new = y_st[group] + DUAL_STEP * (rhs_st[...] - image)
            y_new = jnp.where(kind_st[...] == 1, jnp.maximum(y_new, 0.0), y_new)
            if last:
                from_rows(y_v, group, y_new, y_tiles)
            else:
                y_st[group] = y_new
                gather_start(it + 1, group, y_new, *y_args)
    stores[1].start()
    for it in range(ITERS):
        for group in range(GROUPS):
            drain(y_recv, ys_sem, it, group)
            drain(g_recv, gs_sem, it, group)
            drain(x_recv, xs_sem, it, group)
            if it == ITERS - 1:
                drain_low(hs_sem, it, group)
            else:
                drain(h_recv, hs_sem, it, group)
    for store in stores:
        store.wait()


def body(primal, dual, cost, upper, rhs, row_kind, tiles, tile_rows, tile_cols, tile_count):
    n_row = lax.axis_size("row")
    n_col = lax.axis_size("col")
    x_width, y_width = primal.shape[1], dual.shape[1]
    slots = tiles.shape[0]
    x_rows, y_rows = x_width // 128 * HALF, y_width // 128 * HALF
    any_spec = pl.BlockSpec(memory_space=pl.ANY)
    dma = pltpu.SemaphoreType.DMA
    both = (ITERS, GROUPS)

    def exchange(n, rows):
        return [
            pltpu.VMEM(both + (rows, 128), BF16), pltpu.VMEM(both + (n - 1, rows, 128), BF16),
            pltpu.VMEM(both + (n * rows // HALF, 2 * HALF, 128), F32),
        ]

    def partial(n, rows):
        return [pltpu.VMEM(both + (n, rows, 128), F32), pltpu.VMEM(both + (n - 1, rows, 128), F32)]

    scratch = [
        pltpu.VMEM((8, x_width), F32), pltpu.VMEM((8, y_width), F32), pltpu.VMEM((8, x_width), F32),
        pltpu.VMEM((1, x_width), F32), pltpu.VMEM((1, y_width), F32), pltpu.VMEM((1, y_width), jnp.int32),
        pltpu.VMEM(tiles.shape, BF16), pltpu.VMEM((1, slots), jnp.int32), pltpu.VMEM((1, slots), jnp.int32),
        pltpu.SMEM((1, slots), jnp.int32), pltpu.SMEM((1, slots), jnp.int32),
        pltpu.VMEM((GROUPS, x_rows, 128), F32), pltpu.VMEM((GROUPS, y_rows, 128), F32),
        pltpu.VMEM((GROUPS, x_rows, 128), F32), pltpu.VMEM((x_rows, 128), F32),
        pltpu.VMEM((y_rows, 128), F32), pltpu.VMEM((y_rows, 128), jnp.int32),
        pltpu.VMEM(tiles.shape, BF16),
        pltpu.VMEM((x_rows * n_row, slots * HALF), BF16), pltpu.VMEM((y_rows * n_col, slots * HALF), BF16),
        pltpu.VMEM((GROUPS, slots * HALF, 128), F32),
    ]
    scratch += exchange(n_col, y_rows) + exchange(n_row, x_rows) + partial(n_row, x_rows) + partial(n_col, y_rows)
    scratch += [pltpu.VMEM((GROUPS, n_col, y_rows, 128), BF16), pltpu.VMEM((GROUPS, n_col - 1, y_rows, 128), BF16)]
    scratch += [dma((11,)), dma((2,))] + [dma(both)] * 8
    operands = [
        pltpu.with_memory_space_constraint(operand, pltpu.HBM)
        for operand in (
            primal, dual, cost, upper.reshape(1, -1), rhs.reshape(1, -1), row_kind.reshape(1, -1), tiles,
            tile_rows.reshape(1, -1), tile_cols.reshape(1, -1),
        )
    ]
    return pl.pallas_call(
        functools.partial(kernel, n_row, n_col),
        out_shape=(jax.ShapeDtypeStruct(primal.shape, F32), jax.ShapeDtypeStruct(dual.shape, F32)),
        in_specs=[any_spec] * 9 + [pl.BlockSpec(memory_space=pltpu.SMEM)],
        out_specs=(any_spec, any_spec),
        scratch_shapes=scratch,
        compiler_params=pltpu.CompilerParams(
            collective_id=0, has_side_effects=True, vmem_limit_bytes=40 * 1024 * 1024,
        ),
        name="pdhg",
    )(
        *operands, tile_count,
    )


def solution(mesh):
    in_specs = (
        P(None, ("col", "row")),
        P(None, ("row", "col")),
        P(None, ("col", "row")),
        P(("col", "row")),
        P(("row", "col")),
        P(("row", "col")),
        P(("row", "col"), None, None),
        P(("row", "col")),
        P(("row", "col")),
        P(("row", "col")),
    )
    out_specs = (P(None, ("col", "row")), P(None, ("row", "col")))
    return jax.shard_map(body, mesh=mesh, in_specs=in_specs, out_specs=out_specs, check_vma=False)
```
